256 devices in a mesh: group: 16 (over z, core), dev: 16 (over y, x).
Axes of the slice: x: 4, y: 4, z: 8, core: 2. Of those that a mesh axis runs over, the one named last changes fastest.
Arguments:
- memory: bfloat16 [65536, 512], P(('group', 'dev')), may hold values from -3 to 3
- event_features: bfloat16 [131072, 172], P(('group', 'dev')), may hold values from -6 to 6
- event_dest: int32 [131072, 1], P(('group', 'dev')), may hold values from 0 to 15; in each aligned block of 512 rows (0 to 511, 512 to 1023, ...) at most 96 rows name the same one
- event_slot: int32 [131072], P(('group', 'dev')), may hold values from 0 to 255
- neighbours: int32 [65536, 20], P(('group', 'dev')), may hold values from 0 to 65535, as said below
- w_message: bfloat16 [172, 512], replicated, may hold values from -0.4375 to 0.4375
- w_input: bfloat16 [512, 1536], replicated, may hold values from -0.25 to 0.25
- w_hidden: bfloat16 [512, 1536], replicated, may hold values from -0.25 to 0.25
- w_query: bfloat16 [512, 512], replicated
- w_keyval: bfloat16 [512, 1024], replicated, may hold values from -0.25 to 0.25
- w_output: bfloat16 [512, 512], replicated, may hold values from -0.25 to 0.25
Outputs:
- new_memory: bfloat16 [65536, 512], P(('group', 'dev'))
- embedding: bfloat16 [65536, 512], P(('group', 'dev'))
The draws below stay inside these ranges and needn't reach their ends.
Inputs may be any that keep to these rules, and one draw needn't show every extreme that they name: `event_dest`: every device's 512 events send at most 96 events to one owner, and exactly 96 to some owner. Each cell's neighbours lie in its own range of 4096 cells or in one of the two adjacent ranges, the last range being adjacent to the first. The 5120 entries of one device's cells name cells of each of the 48 owners of these three ranges equally often, up to one, so that no owner is named more than 107 times and some owner exactly 107 times.
All inputs are finite; a program needn't handle non-finite values.
Results may differ from the reference program's by a relative error of at most 0.017.
The reference program's roundings to bfloat16 on the way (of `message`, `mean_msg`, `keyval`, `query`, `attn_w` and `attended`) count: a program that leaves them out, or rounds other values in their place, can miss the bound.
Values may be sent and summed in bfloat16 or wider, within the bound.
A program may use at most 128 MiB of HBM per device.

```python
import math
import jax
import jax.numpy as jnp
import numpy as np
from jax import lax

D = 512
FEAT = 172
HEADS = 8
NBR = 20
CELL_DEV = 256
EV_DEV = 512
HEAD = 64
GROUP_CELLS = 4096
CELLS = 65536
EVENTS = 131072
CAP = 96
N_GROUP = 16
N_DEV = 16


def draw_neighbours(key, part):
    key = jax.random.fold_in(key, 11)
    first, second = jax.random.split(key)
    devices = CELLS // CELL_DEV
    entries = CELL_DEV * NBR
    labels = jnp.arange(entries, dtype=jnp.int32) % (3 * N_DEV)
    device_keys = jax.random.split(first, devices)
    shuffled = jax.vmap(lambda one: jax.random.permutation(one, labels))(device_keys)
    which = shuffled // N_DEV
    owner = shuffled % N_DEV
    device_ids = jnp.arange(devices, dtype=jnp.int32)
    home = (device_ids // N_DEV)[:, None]
    chosen = (home + which - 1 + N_GROUP) % N_GROUP
    inside = jax.random.randint(second, (devices, entries), 0, CELL_DEV)
    result = chosen * GROUP_CELLS + owner * CELL_DEV + inside
    return result.reshape(CELLS, NBR).astype(jnp.int32)


def draw_w_query(key, part):
    key = jax.random.fold_in(key, 23)
    values = jax.random.normal(key, (D, D), jnp.float32) * D ** (-0.5)
    return values.astype(jnp.bfloat16)


def plant(values, rng, smallest, top_value):
    dims = values.shape
    spot = [jax.random.randint(jax.random.fold_in(rng, axis), (), 0, dims[axis]) for axis in range(len(dims))]
    values = values.at[tuple(spot)].set(smallest)
    longest = dims.index(max(dims))
    spot[longest] = (spot[longest] + 1) % dims[longest]
    return values.at[tuple(spot)].set(top_value)


def levels(own_key, shape, cuts, least, high):
    gain = 1.0
    for axis_at, shards_of in cuts:
        heights = jax.random.uniform(jax.random.fold_in(jax.random.fold_in(own_key, 6), axis_at), (shards_of,), jnp.float32, least / len(cuts), high / len(cuts))
        gain = gain * jnp.repeat(jnp.exp(heights), shape[axis_at] // shards_of).reshape((-1,) + (1,) * (len(shape) - 1 - axis_at))
    return gain


def shared_out(own_key, own, number, rows, count, top, most, lean):
    ranking = jax.random.permutation(own_key, count)
    heavy_load, ordinary = load_shares(count, rows * top, most, lean, True), load_shares(count, rows * top, most, lean, False)
    places = jnp.arange(count)

    def named(sizes, rotation):
        used = int((sizes > 0).sum())
        fixed = max(1, used // 4)
        moved = fixed + (places - fixed + rotation * (used - fixed)) % max(1, count - fixed)
        return jnp.zeros((count,), jnp.int32).at[ranking[jnp.where(places < fixed, places, moved)]].set(jnp.asarray(sizes, jnp.int32))

    sizes = jnp.where(number % 4 == 0, named(heavy_load, number // 4), named(ordinary, number - number // 4 - 1))
    mixed = jax.random.permutation(jax.random.fold_in(own, 3), count)
    giver, taker = mixed[0:count // 2 * 2:2], mixed[1:count // 2 * 2:2]
    margin = jnp.minimum(sizes[giver] - 1, most - sizes[taker]) // 2
    margin = jnp.where((giver == ranking[0]) | (taker == ranking[0]) | (sizes[taker] == 0), 0, jnp.maximum(margin, 0))
    moved = jax.random.randint(jax.random.fold_in(own, 4), (count // 2,), 0, 1 << 20) % (margin + 1)
    sizes = sizes.at[giver].add(-moved).at[taker].add(moved)
    items = jnp.searchsorted(jnp.cumsum(sizes), jnp.arange(rows * top), side="right").astype(jnp.int32)
    listing = items.reshape(top, rows).T
    listing = listing[jax.random.permutation(jax.random.fold_in(own, 1), rows)]
    rotation = jax.random.randint(jax.random.fold_in(own, 2), (rows, 1), 0, top)
    return jnp.take_along_axis(listing, (jnp.arange(top)[None, :] + rotation) % top, axis=1)


def load_shares(count, total, reach, slope, full):
    loads = [(1 << 20) // math.isqrt(rank ** slope) + 1 for rank in range(1, count + 1)]
    largest = reach if full else min(reach, max(-(-total // count), total * loads[0] // sum(loads)))
    least = 1 if total - largest >= count - 1 else 0
    holding, spare = [largest] + [least] * (count - 1), total - largest - least * (count - 1)
    while spare > 0:
        free = [i for i in range(1, count) if holding[i] < largest] or [i for i in range(1, count) if holding[i] < reach]
        pool, left = sum([loads[i] for i in free]), spare
        for i in free:
            extra = min(reach - holding[i], max(1, left * loads[i] // pool), spare)
            holding[i] = holding[i] + extra
            spare = spare - extra
    return np.array(holding)


def centred(own_key, extent, spread, limit, cuts=(), held_as=jnp.bfloat16):
    array = jax.random.normal(own_key, extent, jnp.float32) * spread
    if len(cuts) > 0:
        array = levels(own_key, extent, cuts, -0.22, 0.18) * array
    return jnp.clip(array, min=-limit, max=limit).astype(held_as)


def setup_inputs(seed: int = 0) -> dict:
    seeds = jax.random.split(jax.random.key(seed), 12)
    memory = centred(seeds[0], (CELLS, D), 0.5, 3.0, ((0, 256),))
    event_features = centred(seeds[1], (EVENTS, FEAT), 1.0, 6.0, ((0, 256),))
    event_dest_keys = jax.random.split(jax.random.fold_in(seeds[2], 1), EVENTS // EV_DEV)
    event_dest_turns = jax.random.permutation(jax.random.fold_in(seeds[2], 3), EVENTS // EV_DEV)
    event_dest = jax.vmap(lambda own, number: shared_out(jax.random.fold_in(seeds[2], 2), own, number, EV_DEV, N_DEV, 1, CAP, 2))(event_dest_keys, event_dest_turns).reshape((EVENTS, 1))
    event_slot = plant(jax.random.randint(seeds[3], (EVENTS,), 0, CELL_DEV), jax.random.fold_in(seeds[3], 1), 0, CELL_DEV - 1).astype(jnp.int32)
    neighbours = draw_neighbours(jax.random.fold_in(seeds[11], 71), 0)
    w_message = centred(seeds[5], (FEAT, D), FEAT ** -0.5, 0.4375)
    w_input = centred(seeds[6], (D, 3 * D), D ** -0.5, 0.25)
    w_hidden = centred(seeds[7], (D, 3 * D), D ** -0.5, 0.25)
    w_query = draw_w_query(jax.random.fold_in(seeds[11], 71), 0)
    w_keyval = centred(seeds[9], (D, 2 * D), D ** -0.5, 0.25)
    w_output = centred(seeds[10], (D, D), D ** -0.5, 0.25)
    return dict(memory=memory, event_features=event_features, event_dest=event_dest, event_slot=event_slot, neighbours=neighbours, w_message=w_message, w_input=w_input, w_hidden=w_hidden, w_query=w_query, w_keyval=w_keyval, w_output=w_output)


def reference(memory, event_features, event_dest, event_slot, neighbours, w_message, w_input, w_hidden, w_query, w_keyval, w_output):
    rows = jnp.arange(EVENTS, dtype=jnp.int32)
    ranges = rows // (EV_DEV * N_DEV)
    target = (ranges * GROUP_CELLS + event_dest[:, 0] * CELL_DEV + event_slot).astype(jnp.int32)
    message = jax.nn.silu(jnp.dot(event_features, w_message, preferred_element_type=jnp.float32)).astype(jnp.bfloat16)
    sums = jax.ops.segment_sum(message.astype(jnp.float32), target, num_segments=CELLS)
    counts = jax.ops.segment_sum(jnp.ones((EVENTS,), jnp.float32), target, num_segments=CELLS)
    mean_msg = (sums / jnp.maximum(counts, 1.0)[:, None]).astype(jnp.bfloat16)
    gi = jnp.dot(mean_msg, w_input, preferred_element_type=jnp.float32)
    gh = jnp.dot(memory, w_hidden, preferred_element_type=jnp.float32)
    zgate = jax.nn.sigmoid(gi[:, :D] + gh[:, :D])
    rgate = jax.nn.sigmoid(gi[:, D:2 * D] + gh[:, D:2 * D])
    cand = jnp.tanh(gi[:, 2 * D:] + rgate * gh[:, 2 * D:])
    old = memory.astype(jnp.float32)
    updated = (1.0 - zgate) * old + zgate * cand
    new_memory = jnp.where(counts[:, None] > 0, updated, old).astype(jnp.bfloat16)
    keyval = jnp.dot(new_memory, w_keyval, preferred_element_type=jnp.float32).astype(jnp.bfloat16)
    query = (jnp.dot(new_memory, w_query, preferred_element_type=jnp.float32) / jnp.sqrt(jnp.float32(HEAD))).astype(jnp.bfloat16)
    blocks = CELLS // GROUP_CELLS

    def attend(args):
        qblock, nblock, mblock = args
        gathered = jnp.take(keyval, nblock.reshape(-1), axis=0).reshape(GROUP_CELLS, NBR, 2 * D)
        keys = gathered[:, :, :D].reshape(GROUP_CELLS, NBR, HEADS, HEAD).astype(jnp.float32)
        values = gathered[:, :, D:].reshape(GROUP_CELLS, NBR, HEADS, HEAD).astype(jnp.float32)
        qheads = qblock.reshape(GROUP_CELLS, HEADS, HEAD).astype(jnp.float32)
        scores = jnp.einsum('bhd,bnhd->bhn', qheads, keys)
        attn_w = jax.nn.softmax(scores, axis=-1).astype(jnp.bfloat16)
        attended = jnp.einsum('bhn,bnhd->bhd', attn_w.astype(jnp.float32), values).reshape(GROUP_CELLS, D).astype(jnp.bfloat16)
        mixed = mblock.astype(jnp.float32) + jnp.dot(attended, w_output, preferred_element_type=jnp.float32)
        return mixed.astype(jnp.bfloat16)
    embedding = lax.map(attend, (query.reshape(blocks, GROUP_CELLS, D), neighbours.reshape(blocks, GROUP_CELLS, NBR), new_memory.reshape(blocks, GROUP_CELLS, D)))
    return (new_memory, embedding.reshape(CELLS, D))
```

```python
import jax
import jax.numpy as jnp
from jax import lax
from jax.experimental import pallas as pl
from jax.experimental.pallas import tpu as pltpu
from jax.sharding import PartitionSpec as P

MESH = pl.DeviceIdType.MESH
F32, BF16, I32 = jnp.float32, jnp.bfloat16, jnp.int32

HEADS = 8
HEAD = 64
NBR = 20
CELLS = 256
WIDTH = 512
EVENTS = 512
CAP = 96
HALF = CAP // 2
PACK = CAP + HALF
FEAT = 172
TAIL = FEAT - 128
ROWS = 112
LANES = 128
ROLES = 3
OWNERS = 16
SIDE = 4
RANGES = 16
BUCKETS = OWNERS * ROLES
LAG = 2

ORDER = (
    (0, 0), (0, 3), (0, 1), (3, 0), (1, 0), (3, 3), (1, 1), (0, 2),
    (2, 0), (3, 1), (1, 3), (3, 2), (1, 2), (2, 3), (2, 1), (2, 2),
)
SLOT = {rel: slot for slot, rel in enumerate(ORDER)}


def gather_plan():
    names, messages = {}, []

    def add(name, source, hop, first, rows):
        target = ((source[0] - hop[0]) % SIDE, (source[1] - hop[1]) % SIDE)
        names[name] = len(messages)
        messages.append((SLOT[source], SLOT[target], first, rows, hop))

    for cls in "ab":
        base = 0 if cls == "a" else 128

        def at(first, second, cls=cls):
            return (second % SIDE, first % SIDE) if cls == "a" else (first % SIDE, second % SIDE)

        for sign in (1, -1):
            add((cls, 1, 0, sign), at(0, 0), at(sign, 0), base, 128)
            add((cls, 2, 0, sign), at(-sign, 0), at(sign, 0), base + (0 if sign > 0 else 64), 64)
            for off in (0, -1, 1, 2):
                add((cls, 3, off, sign), at(off, 0), at(0, sign), base, 128)
                first = base + (0 if sign > 0 else 64)
                add((cls, 4, off, sign), at(off, -sign), at(0, sign), first, 64)

    def both(*items):
        return [names[(cls,) + item] for item in items for cls in "ab"]

    start = both((1, 0, 1), (1, 0, -1), (3, 0, 1), (3, 0, -1))
    steps = {
        1: [
            (
                both((1, 0, 1), (1, 0, -1)),
                both((2, 0, 1), (2, 0, -1), (3, -1, 1), (3, 1, -1)),
            ),
            (
                both((3, 0, 1), (3, 0, -1)),
                both((4, 0, 1), (4, 0, -1), (3, 1, 1), (3, -1, -1)),
            ),
        ],
        3: [(both((2, 0, 1), (2, 0, -1)), both((3, 2, 1), (3, 2, -1)))],
        5: [(both((3, -1, 1)), both((4, -1, 1)))],
        6: [(both((3, 1, -1)), both((4, 1, -1)))],
        7: [([names[("b", 4, 0, 1)], names[("b", 4, 0, -1)]], [])],
        8: [([names[("a", 4, 0, 1)], names[("a", 4, 0, -1)]], [])],
        9: [
            (
                [names[("a", 3, 1, 1)], names[("b", 3, -1, -1)]],
                [names[("a", 4, 1, 1)], names[("b", 4, -1, -1)]],
            )
        ],
        10: [
            (
                [names[("a", 3, -1, -1)], names[("b", 3, 1, 1)]],
                [names[("a", 4, -1, -1)], names[("b", 4, 1, 1)]],
            )
        ],
        11: [
            (both((3, 2, 1), (3, 2, -1)), both((4, 2, 1), (4, 2, -1))),
            ([names[("b", 4, -1, 1)], names[("b", 4, -1, -1)]], []),
        ],
        12: [([names[("b", 4, 1, 1)], names[("b", 4, 1, -1)]], [])],
        13: [([names[("a", 4, -1, 1)], names[("a", 4, -1, -1)]], [])],
        14: [([names[("a", 4, 1, 1)], names[("a", 4, 1, -1)]], [])],
        15: [(both((4, 2, 1), (4, 2, -1)), [])],
    }
    return messages, start, steps


MESSAGES, START, STEPS = gather_plan()
COUNT = len(MESSAGES)


def iota(shape, dim):
    return lax.broadcasted_iota(I32, shape, dim)


def dot(a, b):
    return jnp.dot(a, b, preferred_element_type=F32)


def dot_nt(a, b):
    return lax.dot_general(a, b, (((1,), (1,)), ((), ())), preferred_element_type=F32)


def dot_tn(a, b):
    return lax.dot_general(a, b, (((0,), (0,)), ((), ())), preferred_element_type=F32)


def ones_where(mask):
    return jnp.where(mask, 1.0, 0.0).astype(BF16)


def sigmoid(x):
    return 0.5 * jnp.tanh(0.5 * x) + 0.5


def kernel(
    mem_ref, feat_ref, dest_ref, slot_ref, nbr_ref, wmsg_ref,
    win_hbm, whid_hbm, wq_hbm, wkv_hbm, wout_hbm,
    new_ref, emb_ref,
    win, whid, wq, wkv, wout,
    tail, wtail, ev_out, ev_in, gh, sums, cnt,
    bkt, ind, tabs, reqs, celltab, cmat,
    blocks, picks, to_left, to_right, q_ref, vals, scores, probs, spread,
    w_sem, ev_send, ev_recv, rq_send, rq_recv, bl_send, bl_recv, pk_send, pk_recv,
):
    group, dev = lax.axis_index("group"), lax.axis_index("dev")
    y, x = dev // SIDE, dev % SIDE
    left, right = (group + RANGES - 1) % RANGES, (group + 1) % RANGES

    def owner(dy, dx):
        return ((y + dy) % SIDE) * SIDE + (x + dx) % SIDE

    barrier = pltpu.get_barrier_semaphore()

    def greet(k, _):
        pl.semaphore_signal(
            barrier, inc=1, device_id=(group, owner(k // SIDE, k % SIDE)), device_id_type=MESH
        )
        return 0

    lax.fori_loop(1, OWNERS, greet, 0)
    for side in (left, right):
        pl.semaphore_signal(barrier, inc=1, device_id=(side, dev), device_id_type=MESH)

    loads = [
        pltpu.make_async_copy(src, dst, w_sem.at[i])
        for i, (src, dst) in enumerate(
            ((whid_hbm, whid), (win_hbm, win), (wq_hbm, wq), (wkv_hbm, wkv), (wout_hbm, wout))
        )
    ]
    for load in loads:
        load.start()

    tail[...] = jnp.zeros_like(tail)
    tail[0:TAIL, :] = feat_ref[128:FEAT, :].astype(F32)
    tail[TAIL : TAIL + 1, :] = (slot_ref[...] + 1).astype(F32)
    tails = tail[...].astype(BF16)
    blank = jnp.zeros((64, EVENTS), BF16)
    tails_lo = jnp.concatenate([tails, blank], axis=0)
    tails_hi = jnp.concatenate([blank, tails], axis=0)
    head = feat_ref[0:128, :]
    dest = dest_ref[...]
    mine = iota((OWNERS, EVENTS), 0) == dest
    upper = ones_where(iota((EVENTS, EVENTS), 0) < iota((EVENTS, EVENTS), 1))
    before = dot(ones_where(mine), upper)
    place = jnp.sum(jnp.where(mine, before, 0.0), axis=0, keepdims=True).astype(I32) + dest * CAP

    pl.semaphore_wait(barrier, OWNERS - 1 + 2)

    def ev_copy(k):
        return pltpu.make_async_remote_copy(
            src_ref=ev_out.at[k],
            dst_ref=ev_in.at[k],
            send_sem=ev_send.at[k],
            recv_sem=ev_recv.at[k],
            device_id=(group, owner(k // SIDE, k % SIDE)),
            device_id_type=MESH,
        )

    def pack(i, _):
        k = OWNERS - 1 - i
        pick = ones_where(iota((CAP, EVENTS), 0) == place - owner(k // SIDE, k % SIDE) * CAP)
        ev_out[k, 0:CAP, :] = dot_nt(pick, head).astype(BF16)
        ev_out[k, CAP:PACK, :] = (
            dot_nt(pick[0:HALF], tails_lo) + dot_nt(pick[HALF:CAP], tails_hi)
        ).astype(BF16)

        @pl.when(k > 0)
        def _():
            ev_copy(k).start()

        return 0

    lax.fori_loop(0, OWNERS, pack, 0)
    ev_in[0] = ev_out[0]

    ids = nbr_ref[...]
    role = ((ids >> 12) - group + 1 + RANGES) % RANGES
    named = (ids >> 8) & 15
    rel = (((named >> 2) - y) & 3) * SIDE + ((named - x) & 3)
    slot_of = jnp.zeros_like(rel)
    for number, (dy, dx) in enumerate(ORDER):
        slot_of = jnp.where(rel == dy * SIDE + dx, number, slot_of)
    bucket = slot_of * ROLES + role
    bkt[...] = bucket
    wanted = (ids & 255) + 1
    cell = iota((1, CELLS), 1) + 1
    ahead = ones_where(iota((CELLS, CELLS), 0) < iota((CELLS, CELLS), 1))
    offset = jnp.zeros((BUCKETS, 1), F32)
    bucket_ids, place_ids = iota((BUCKETS, CELLS), 0), iota((LANES, CELLS), 0)
    table = jnp.zeros((LANES, LANES), F32)
    cells_of = jnp.zeros((BUCKETS, LANES), F32)
    for j in range(NBR):
        inside = bucket_ids == bucket[j : j + 1, :]
        rank = dot(ones_where(inside), ahead) + offset
        offset = offset + jnp.sum(jnp.where(inside, 1.0, 0.0), axis=1, keepdims=True)
        rank = jnp.sum(jnp.where(inside, rank, 0.0), axis=0, keepdims=True).astype(I32)
        hot = ones_where(place_ids == rank)
        ind[0:LANES, j * CELLS : (j + 1) * CELLS] = hot
        ind[LANES : 2 * LANES, j * CELLS : (j + 1) * CELLS] = hot
        asked = jnp.where(inside, wanted[j : j + 1, :].astype(F32), 0.0).astype(BF16)
        by = jnp.where(inside, cell.astype(F32), 0.0).astype(BF16)
        both = jnp.concatenate([asked, by, jnp.zeros((LANES - 2 * BUCKETS, CELLS), BF16)], axis=0)
        table = table + dot_nt(hot, both)
        cells_of = cells_of + dot_nt(by, hot)
    tabs[...] = table.astype(BF16)
    celltab[...] = cells_of

    asks = [
        pltpu.make_async_remote_copy(
            src_ref=tabs,
            dst_ref=reqs.at[i],
            send_sem=rq_send.at[i],
            recv_sem=rq_recv.at[i],
            device_id=(side, dev),
            device_id_type=MESH,
        )
        for i, side in enumerate((right, left))
    ]
    for ask in asks:
        ask.start()

    loads[0].wait()
    memory = mem_ref[...]
    for part in range(3):
        columns = slice(part * WIDTH, (part + 1) * WIDTH)
        gh[:, columns] = dot(memory, whid[:, columns])

    def cell_matrix(s, _):
        for r in range(ROLES):
            row = celltab[pl.ds(s * ROLES + r, 1), :]
            hot = ones_where((iota((CELLS, LANES), 0) + 1).astype(F32) == row)
            cmat[s, :, r * LANES : (r + 1) * LANES] = hot
            vals[s, r * LANES + ROWS : (r + 1) * LANES, :] = jnp.zeros((LANES - ROWS, WIDTH), BF16)
        return 0

    lax.fori_loop(0, OWNERS, cell_matrix, 0)
    scores[...] = jnp.zeros_like(scores)
    wtail[...] = jnp.zeros_like(wtail)
    wtail[0:TAIL, :] = wmsg_ref[128:FEAT, :].astype(F32)
    w_tail = wtail[...].astype(BF16)
    w_blank = jnp.zeros((64, WIDTH), BF16)
    w_lo = jnp.concatenate([wmsg_ref[0:128, :], w_tail, w_blank], axis=0)
    w_hi = jnp.concatenate([wmsg_ref[0:128, :], w_blank, w_tail], axis=0)

    sums[...] = jnp.zeros_like(sums)
    cnt[...] = jnp.zeros_like(cnt)
    for chunk in (1, 0):
        first = chunk * 8

        def arrived(k, _):
            ev_copy(k).wait_recv()
            return 0

        lax.fori_loop(max(first, 1), first + 8, arrived, 0)
        tail_in = ev_in[first : first + 8, CAP:PACK, :].reshape(8 * HALF, 128)
        for part, weights in enumerate((w_lo, w_hi)):
            main = ev_in[first : first + 8, part * HALF : (part + 1) * HALF, :].reshape(
                8 * HALF, 128
            )
            raw = dot(jnp.concatenate([main, tail_in], axis=1), weights)
            message = (raw * sigmoid(raw)).astype(BF16)
            column = ones_where(iota((16, 128), 1) == 64 * part + TAIL)
            marks = dot_nt(column, tail_in)[0:1, :]
            here = (iota((CELLS, 8 * HALF), 0) + 1).astype(F32) == marks
            sums[...] += dot(ones_where(here), message)
            cnt[...] += jnp.sum(jnp.where(here, 1.0, 0.0), axis=1, keepdims=True)

    counts = cnt[:, 0:1]
    mean_msg = (sums[...] / jnp.maximum(counts, 1.0)).astype(BF16)
    loads[1].wait()
    gate_z = sigmoid(dot(mean_msg, win[:, 0:WIDTH]) + gh[:, 0:WIDTH])
    gate_r = sigmoid(dot(mean_msg, win[:, WIDTH : 2 * WIDTH]) + gh[:, WIDTH : 2 * WIDTH])
    cand = jnp.tanh(dot(mean_msg, win[:, 2 * WIDTH :]) + gate_r * gh[:, 2 * WIDTH :])
    old = memory.astype(F32)
    updated = (1.0 - gate_z) * old + gate_z * cand
    new_memory = jnp.where(counts > 0, updated, old).astype(BF16)
    blocks[0] = new_memory
    new_ref[...] = new_memory

    def bl_copy(number):
        source, target, first, rows, (dy, dx) = MESSAGES[number]
        return pltpu.make_async_remote_copy(
            src_ref=blocks.at[source, pl.ds(first, rows)],
            dst_ref=blocks.at[target, pl.ds(first, rows)],
            send_sem=bl_send.at[number],
            recv_sem=bl_recv.at[number],
            device_id=(group, owner(dy, dx)),
            device_id_type=MESH,
        )

    def pk_copy(side, s):
        source, first, target = ((to_right, 0, right), (to_left, 2 * ROWS, left))[side]
        return pltpu.make_async_remote_copy(
            src_ref=source.at[s],
            dst_ref=picks.at[s, pl.ds(first, ROWS)],
            send_sem=pk_send.at[side, s],
            recv_sem=pk_recv.at[side, s],
            device_id=(target, dev),
            device_id_type=MESH,
        )

    for number in START:
        bl_copy(number).start()
    loads[2].wait()
    q_ref[...] = (dot(new_memory, wq[...]) * (HEAD**-0.5)).astype(BF16)
    for ask in asks:
        ask.wait_recv()
    loads[3].wait()

    def chosen(tab, column):
        select = ones_where(iota((LANES, CELLS), 0) == column)
        values = dot(tab, select)
        return ones_where(values == (iota((ROWS, CELLS), 1) + 1).astype(F32))

    head_rows = ones_where(iota((16, WIDTH), 0) == iota((16, WIDTH), 1) // HEAD)

    def step(s, _):
        @pl.when(s < OWNERS)
        def _():
            for at, stages in STEPS.items():

                @pl.when(s == at)
                def _(stages=stages):
                    for awaited, sent in stages:
                        for number in awaited:
                            bl_copy(number).wait_recv()
                        for number in sent:
                            bl_copy(number).start()

            block = blocks[s]
            for_right = chosen(reqs[1, 0:ROWS, :], s * ROLES)
            for_left = chosen(reqs[0, 0:ROWS, :], s * ROLES + 2)
            for_own = chosen(tabs[0:ROWS, :], s * ROLES + 1)
            got = dot(jnp.concatenate([for_right, for_left, for_own], axis=0), block).astype(BF16)
            to_right[s] = got[0:ROWS]
            pk_copy(0, s).start()
            to_left[s] = got[ROWS : 2 * ROWS]
            pk_copy(1, s).start()
            picks[s, ROWS : 2 * ROWS, :] = got[2 * ROWS : 3 * ROWS]

        @pl.when(s >= LAG)
        def _():
            t = s - LAG
            for side in range(2):
                pk_copy(side, t).wait_recv()
            keyval = dot(picks[t], wkv[...])
            owned = jnp.concatenate(
                [
                    chosen(tabs[0:ROWS, :], BUCKETS + t * ROLES + r)
                    for r in range(ROLES)
                ],
                axis=0,
            )
            product = dot(owned, q_ref[...]) * keyval[:, 0:WIDTH].astype(BF16).astype(F32)
            upper_part = product.astype(BF16)
            lower_part = (product - upper_part.astype(F32)).astype(BF16)
            values = keyval[:, WIDTH:].astype(BF16)
            for r in range(ROLES):
                rows = slice(r * ROWS, (r + 1) * ROWS)
                score = dot_nt(head_rows, upper_part[rows]) + dot_nt(head_rows, lower_part[rows])
                first = pl.multiple_of((t * ROLES + r) * HEADS, HEADS)
                scores[pl.ds(first, HEADS), 0:ROWS] = score[0:HEADS]
                vals[t, r * LANES : r * LANES + ROWS, :] = values[rows]

        return 0

    lax.fori_loop(0, OWNERS + LAG, step, 0)

    all_scores = scores[...]
    upper_part = all_scores.astype(BF16)
    lower_part = (all_scores - upper_part.astype(F32)).astype(BF16)
    parts = jnp.concatenate([upper_part, lower_part], axis=1)
    numbers = lax.broadcasted_iota(I32, (BUCKETS, HEADS, CELLS), 0)
    for j in range(NBR):
        found = dot(parts, ind[:, j * CELLS : (j + 1) * CELLS]).reshape(BUCKETS, HEADS, CELLS)
        inside = numbers == bkt[j : j + 1, :].reshape(1, 1, CELLS)
        probs[j] = jnp.sum(jnp.where(inside, found, 0.0), axis=0)
    top = probs[0]
    for j in range(1, NBR):
        top = jnp.maximum(top, probs[j])
    total = jnp.zeros_like(top)
    for j in range(NBR):
        raised = jnp.exp(probs[j] - top)
        probs[j] = raised
        total = total + raised
    inverse = 1.0 / total
    for j in range(NBR):
        weight = (probs[j] * inverse).astype(BF16).astype(F32)
        inside = numbers == bkt[j : j + 1, :].reshape(1, 1, CELLS)
        placed = jnp.where(inside, weight[None], 0.0).reshape(BUCKETS * HEADS, CELLS)
        spread[:, j * CELLS : (j + 1) * CELLS] = placed.astype(BF16)
    scores[...] = dot_nt(spread[...], ind[0:LANES, :])

    sums[...] = jnp.zeros_like(sums)
    widen = ones_where(iota((HEADS, WIDTH), 0) == iota((HEADS, WIDTH), 1) // HEAD)

    def weigh(s, _):
        weighted = []
        for r in range(ROLES):
            first = pl.multiple_of((s * ROLES + r) * HEADS, HEADS)
            wide = dot_tn(scores[pl.ds(first, HEADS), :].astype(BF16), widen)
            value = vals[s, r * LANES : (r + 1) * LANES, :].astype(F32)
            weighted.append((wide * value).astype(BF16))
        sums[...] += dot(cmat[s], jnp.concatenate(weighted, axis=0))
        return 0

    lax.fori_loop(0, OWNERS, weigh, 0)
    attended = sums[...].astype(BF16)
    loads[4].wait()
    emb_ref[...] = (blocks[0].astype(F32) + dot(attended, wout[...])).astype(BF16)

    def sent(k, _):
        ev_copy(k).wait_send()
        return 0

    lax.fori_loop(1, OWNERS, sent, 0)
    for ask in asks:
        ask.wait_send()
    for number in range(COUNT):
        bl_copy(number).wait_send()

    def given(s, _):
        for side in range(2):
            pk_copy(side, s).wait_send()
        return 0

    lax.fori_loop(0, OWNERS, given, 0)


def body(memory, features, dest, slot, neighbours, w_message, w_input, w_hidden, w_query, w_keyval, w_output):
    inside = pl.BlockSpec(memory_space=pltpu.VMEM)
    outside = pl.BlockSpec(memory_space=pl.ANY)
    vmem, dma = pltpu.VMEM, pltpu.SemaphoreType.DMA
    return pl.pallas_call(
        kernel,
        out_shape=(
            jax.ShapeDtypeStruct((CELLS, WIDTH), BF16),
            jax.ShapeDtypeStruct((CELLS, WIDTH), BF16),
        ),
        in_specs=[inside] * 6 + [outside] * 5,
        out_specs=(inside, inside),
        scratch_shapes=[
            vmem((WIDTH, 3 * WIDTH), BF16),
            vmem((WIDTH, 3 * WIDTH), BF16),
            vmem((WIDTH, WIDTH), BF16),
            vmem((WIDTH, 2 * WIDTH), BF16),
            vmem((WIDTH, WIDTH), BF16),
            vmem((64, EVENTS), F32),
            vmem((64, WIDTH), F32),
            vmem((OWNERS, PACK, 128), BF16),
            vmem((OWNERS, PACK, 128), BF16),
            vmem((CELLS, 3 * WIDTH), F32),
            vmem((CELLS, WIDTH), F32),
            vmem((CELLS, LANES), F32),
            vmem((NBR, CELLS), I32),
            vmem((2 * LANES, NBR * CELLS), BF16),
            vmem((LANES, LANES), BF16),
            vmem((2, LANES, LANES), BF16),
            vmem((BUCKETS, LANES), F32),
            vmem((OWNERS, CELLS, ROLES * LANES), BF16),
            vmem((OWNERS, CELLS, WIDTH), BF16),
            vmem((OWNERS, ROLES * ROWS, WIDTH), BF16),
            vmem((OWNERS, ROWS, WIDTH), BF16),
            vmem((OWNERS, ROWS, WIDTH), BF16),
            vmem((CELLS, WIDTH), BF16),
            vmem((OWNERS, ROLES * LANES, WIDTH), BF16),
            vmem((BUCKETS * HEADS, LANES), F32),
            vmem((NBR, HEADS, CELLS), F32),
            vmem((BUCKETS * HEADS, NBR * CELLS), BF16),
            dma((5,)),
            dma((OWNERS,)),
            dma((OWNERS,)),
            dma((2,)),
            dma((2,)),
            dma((COUNT,)),
            dma((COUNT,)),
            dma((2, OWNERS)),
            dma((2, OWNERS)),
        ],
        compiler_params=pltpu.CompilerParams(
            collective_id=0, has_side_effects=True, vmem_limit_bytes=58 * 1024 * 1024
        ),
        cost_estimate=pl.CostEstimate(
            flops=12_000_000_000, bytes_accessed=6_000_000, transcendentals=2_000_000
        ),
    )(
        memory,
        features.T,
        dest.reshape(1, EVENTS),
        slot.reshape(1, EVENTS),
        neighbours.T,
        w_message,
        w_input,
        w_hidden,
        w_query,
        w_keyval,
        w_output,
    )


def solution(mesh):
    rows = P(("group", "dev"), None)
    placed = (rows, rows, rows, P(("group", "dev")), rows) + (P(),) * 6
    return jax.shard_map(
        body, mesh=mesh, in_specs=placed, out_specs=(rows, rows), check_vma=False
    )
```

```python
import jax
import jax.numpy as jnp
from jax import lax
from jax.experimental import pallas as pl
from jax.experimental.pallas import tpu as pltpu
from jax.sharding import PartitionSpec as P

MESH = pl.DeviceIdType.MESH
F32, BF16, I32 = jnp.float32, jnp.bfloat16, jnp.int32

HEADS = 8
HEAD = 64
NBR = 20
CELLS = 256
WIDTH = 512
EVENTS = 512
CAP = 96
HALF = CAP // 2
PACK = CAP + HALF
FEAT = 172
TAIL = FEAT - 128
ROWS = 112
LANES = 128
ROLES = 3
OWNERS = 16
SIDE = 4
RANGES = 16
BUCKETS = OWNERS * ROLES
TILE = 256
LAG = 5
BATCH = 4

ORDER = (
    (0, 0), (0, 3), (0, 1), (3, 0), (1, 0), (3, 3), (1, 1), (0, 2),
    (2, 0), (3, 1), (1, 3), (3, 2), (1, 2), (2, 3), (2, 1), (2, 2),
)
SLOT = {rel: slot for slot, rel in enumerate(ORDER)}


def gather_plan():
    names, messages = {}, []

    def add(name, source, hop, first, rows):
        target = ((source[0] - hop[0]) % SIDE, (source[1] - hop[1]) % SIDE)
        names[name] = len(messages)
        messages.append((SLOT[source], SLOT[target], first, rows, hop))

    for cls in "ab":
        base = 0 if cls == "a" else 128

        def at(first, second, cls=cls):
            return (second % SIDE, first % SIDE) if cls == "a" else (first % SIDE, second % SIDE)

        for sign in (1, -1):
            add((cls, 1, 0, sign), at(0, 0), at(sign, 0), base, 128)
            add((cls, 2, 0, sign), at(-sign, 0), at(sign, 0), base + (0 if sign > 0 else 64), 64)
            for off in (0, -1, 1, 2):
                add((cls, 3, off, sign), at(off, 0), at(0, sign), base, 128)
                first = base + (0 if sign > 0 else 64)
                add((cls, 4, off, sign), at(off, -sign), at(0, sign), first, 64)

    def both(*items):
        return [names[(cls,) + item] for item in items for cls in "ab"]

    start = both((1, 0, 1), (1, 0, -1), (3, 0, 1), (3, 0, -1))
    steps = {
        1: [
            (
                both((1, 0, 1), (1, 0, -1)),
                both((2, 0, 1), (2, 0, -1), (3, -1, 1), (3, 1, -1)),
            ),
            (
                both((3, 0, 1), (3, 0, -1)),
                both((4, 0, 1), (4, 0, -1), (3, 1, 1), (3, -1, -1)),
            ),
        ],
        3: [(both((2, 0, 1), (2, 0, -1)), both((3, 2, 1), (3, 2, -1)))],
        5: [(both((3, -1, 1)), both((4, -1, 1)))],
        6: [(both((3, 1, -1)), both((4, 1, -1)))],
        7: [([names[("b", 4, 0, 1)], names[("b", 4, 0, -1)]], [])],
        8: [([names[("a", 4, 0, 1)], names[("a", 4, 0, -1)]], [])],
        9: [
            (
                [names[("a", 3, 1, 1)], names[("b", 3, -1, -1)]],
                [names[("a", 4, 1, 1)], names[("b", 4, -1, -1)]],
            )
        ],
        10: [
            (
                [names[("a", 3, -1, -1)], names[("b", 3, 1, 1)]],
                [names[("a", 4, -1, -1)], names[("b", 4, 1, 1)]],
            )
        ],
        11: [
            (both((3, 2, 1), (3, 2, -1)), both((4, 2, 1), (4, 2, -1))),
            ([names[("b", 4, -1, 1)], names[("b", 4, -1, -1)]], []),
        ],
        12: [([names[("b", 4, 1, 1)], names[("b", 4, 1, -1)]], [])],
        13: [([names[("a", 4, -1, 1)], names[("a", 4, -1, -1)]], [])],
        14: [([names[("a", 4, 1, 1)], names[("a", 4, 1, -1)]], [])],
        15: [(both((4, 2, 1), (4, 2, -1)), [])],
    }
    return messages, start, steps


MESSAGES, START, STEPS = gather_plan()
COUNT = len(MESSAGES)
GROUPS = [awaited for stages in STEPS.values() for awaited, _ in stages]
GROUP_OF = {number: group for group, awaited in enumerate(GROUPS) for number in awaited}
SENT_BLOCKS = sum(message[3] for message in MESSAGES) // CELLS


def iota(shape, dim):
    return lax.broadcasted_iota(I32, shape, dim)


def dot(a, b):
    return jnp.dot(a, b, preferred_element_type=F32)


def dot_nt(a, b):
    return lax.dot_general(a, b, (((1,), (1,)), ((), ())), preferred_element_type=F32)


def dot_tn(a, b):
    return lax.dot_general(a, b, (((0,), (0,)), ((), ())), preferred_element_type=F32)


def ones_where(mask):
    return jnp.where(mask, 1.0, 0.0).astype(BF16)


def sigmoid(x):
    return 0.5 * jnp.tanh(0.5 * x) + 0.5


def kernel(
    mem_ref, feat_ref, dest_ref, slot_ref, nbr_ref, wmsg_ref,
    win_hbm, whid_hbm, wq_hbm, wkv_hbm, wout_hbm,
    new_ref, emb_ref,
    win, whid, wq, wkv, wout,
    tail, wtail, ev_out, ev_in, gh, sums, cnt,
    mean_msg, w_both, row_hot, cell_hot, bkt, wanted, table, ind, tabs, reqs, celltab, cmat,
    blocks, picks, to_left, to_right, q_ref, vals, scores, probs,
    w_sem, ev_send, ev_recv, rq_send, rq_recv, bl_send, bl_recv, pk_send, pk_recv,
):
    group, dev = lax.axis_index("group"), lax.axis_index("dev")
    y, x = dev // SIDE, dev % SIDE
    left, right = (group + RANGES - 1) % RANGES, (group + 1) % RANGES

    def owner(dy, dx):
        return ((y + dy) % SIDE) * SIDE + (x + dx) % SIDE

    def finish(part, sem):
        pltpu.make_async_copy(part, part, sem).wait()

    barrier = pltpu.get_barrier_semaphore()

    def greet(k, _):
        pl.semaphore_signal(
            barrier, inc=1, device_id=(group, owner(k // SIDE, k % SIDE)), device_id_type=MESH
        )
        return 0

    lax.fori_loop(1, OWNERS, greet, 0)
    for side in (left, right):
        pl.semaphore_signal(barrier, inc=1, device_id=(side, dev), device_id_type=MESH)

    loads = [
        pltpu.make_async_copy(src, dst, w_sem.at[i])
        for i, (src, dst) in enumerate(
            ((whid_hbm, whid), (win_hbm, win), (wq_hbm, wq), (wkv_hbm, wkv), (wout_hbm, wout))
        )
    ]
    for load in loads:
        load.start()

    tail[...] = jnp.zeros_like(tail)
    tail[0:TAIL, :] = feat_ref[128:FEAT, :].astype(F32)
    tail[TAIL : TAIL + 1, :] = (slot_ref[...] + 1).astype(F32)
    tails = tail[...].astype(BF16)
    blank = jnp.zeros((64, EVENTS), BF16)
    head = feat_ref[0:128, :]
    feats = (
        jnp.concatenate([head, tails, blank], axis=0),
        jnp.concatenate([head, blank, tails], axis=0),
    )
    dest = dest_ref[...]
    mine = iota((OWNERS, EVENTS), 0) == dest
    upper = ones_where(iota((EVENTS, EVENTS), 0) < iota((EVENTS, EVENTS), 1))
    before = dot(ones_where(mine), upper)
    place = jnp.sum(jnp.where(mine, before, 0.0), axis=0, keepdims=True).astype(I32) + dest * CAP

    def ev_copy(k):
        return pltpu.make_async_remote_copy(
            src_ref=ev_out.at[k],
            dst_ref=ev_in.at[k],
            send_sem=ev_send.at[0],
            recv_sem=ev_recv.at[k // 8],
            device_id=(group, owner(k // SIDE, k % SIDE)),
            device_id_type=MESH,
        )

    def pack(i, _):
        rows = SIDE - 1 - i
        packed = []
        for part in range(2):
            pick = [
                iota((HALF, EVENTS), 0) == place - (owner(rows, column) * CAP + part * HALF)
                for column in range(SIDE)
            ]
            pick = jnp.concatenate([ones_where(one) for one in pick], axis=0)
            packed.append(dot_nt(pick, feats[part]))
        for column in range(SIDE):
            k = rows * SIDE + column
            at = slice(column * HALF, (column + 1) * HALF)
            ev_out[k, 0:HALF, :] = packed[0][at, 0:128].astype(BF16)
            ev_out[k, HALF:CAP, :] = packed[1][at, 0:128].astype(BF16)
            ev_out[k, CAP:PACK, :] = (packed[0][at, 128:] + packed[1][at, 128:]).astype(BF16)
        return 0

    lax.fori_loop(0, SIDE, pack, 0)
    ev_in[0] = ev_out[0]
    pl.semaphore_wait(barrier, OWNERS - 1 + 2)

    def send_events(i, _):
        ev_copy(OWNERS - 1 - i).start()
        return 0

    lax.fori_loop(0, OWNERS - 1, send_events, 0)

    ids = nbr_ref[...]
    role = ((ids >> 12) - group + 1 + RANGES) % RANGES
    named = (ids >> 8) & 15
    rel = (((named >> 2) - y) & 3) * SIDE + ((named - x) & 3)
    slot_of = jnp.zeros_like(rel)
    for number, (dy, dx) in enumerate(ORDER):
        slot_of = jnp.where(rel == dy * SIDE + dx, number, slot_of)
    bucket = slot_of * ROLES + role
    bkt[...] = bucket
    wanted[...] = (ids & 255) + 1
    ahead = ones_where(iota((CELLS, CELLS), 0) < iota((CELLS, CELLS), 1))
    bucket_ids, place_ids = iota((BUCKETS, CELLS), 0), iota((LANES, CELLS), 0)
    cell = jnp.broadcast_to((iota((1, CELLS), 1) + 1).astype(F32), (BUCKETS, CELLS))
    filler = jnp.zeros((LANES - 2 * BUCKETS, CELLS), BF16)
    table[...] = jnp.zeros_like(table)

    def tabulate(i, offset):
        inside = [bucket_ids == bkt[pl.ds(i * BATCH + j, 1), :] for j in range(BATCH)]
        before = dot(jnp.concatenate([ones_where(one) for one in inside], axis=0), ahead)
        hots, boths = [], []
        for j in range(BATCH):
            rank = before[j * BUCKETS : (j + 1) * BUCKETS] + offset
            offset = offset + jnp.sum(jnp.where(inside[j], 1.0, 0.0), axis=1, keepdims=True)
            rank = jnp.sum(jnp.where(inside[j], rank, 0.0), axis=0, keepdims=True).astype(I32)
            hot = ones_where(place_ids == rank)
            at = pl.ds(pl.multiple_of((i * BATCH + j) * CELLS, CELLS), CELLS)
            ind[0:LANES, at] = hot
            ind[LANES : 2 * LANES, at] = hot
            row = wanted[pl.ds(i * BATCH + j, 1), :].astype(F32)
            asked = jnp.where(inside[j], row, 0.0).astype(BF16)
            by = jnp.where(inside[j], cell, 0.0).astype(BF16)
            hots.append(hot)
            boths.append(jnp.concatenate([asked, by, filler], axis=0))
        table[...] += dot_nt(jnp.concatenate(hots, axis=1), jnp.concatenate(boths, axis=1))
        return offset

    lax.fori_loop(0, NBR // BATCH, tabulate, jnp.zeros((BUCKETS, 1), F32))
    tabs[...] = table[...].astype(BF16)
    celltab[...] = table[...].T[BUCKETS : 2 * BUCKETS, :]

    asks = [
        pltpu.make_async_remote_copy(
            src_ref=tabs,
            dst_ref=reqs.at[i],
            send_sem=rq_send.at[i],
            recv_sem=rq_recv.at[i],
            device_id=(side, dev),
            device_id_type=MESH,
        )
        for i, side in enumerate((right, left))
    ]
    for ask in asks:
        ask.start()

    def chosen(tab, column):
        select = ones_where(iota((LANES, CELLS), 0) == column)
        values = dot(tab[0:ROWS, :], select)
        return ones_where(values == (iota((ROWS, CELLS), 1) + 1).astype(F32))

    def cell_matrix(s, _):
        for r in range(ROLES):
            row = celltab[pl.ds(s * ROLES + r, 1), :]
            hot = ones_where((iota((CELLS, LANES), 0) + 1).astype(F32) == row)
            cmat[s, :, r * LANES : (r + 1) * LANES] = hot
            cell_hot[s, r * ROWS : (r + 1) * ROWS, :] = chosen(tabs, BUCKETS + s * ROLES + r)
            vals[s, r * LANES + ROWS : (r + 1) * LANES, :] = jnp.zeros((LANES - ROWS, WIDTH), BF16)
        row_hot[s, 2 * ROWS : 3 * ROWS, :] = chosen(tabs, s * ROLES + 1)
        return 0

    lax.fori_loop(0, OWNERS, cell_matrix, 0)
    scores[...] = jnp.zeros_like(scores)
    loads[0].wait()

    def hidden(part, _):
        columns = pl.ds(pl.multiple_of(part * WIDTH, WIDTH), WIDTH)
        gh[:, columns] = dot(mem_ref[...], whid[:, columns])
        return 0

    lax.fori_loop(0, 3, hidden, 0)

    wtail[...] = jnp.zeros_like(wtail)
    wtail[0:TAIL, :] = wmsg_ref[128:FEAT, :].astype(F32)
    w_tail = wtail[...].astype(BF16)
    w_blank = jnp.zeros((64, WIDTH), BF16)
    w_both[0] = jnp.concatenate([wmsg_ref[0:128, :], w_tail, w_blank], axis=0)
    w_both[1] = jnp.concatenate([wmsg_ref[0:128, :], w_blank, w_tail], axis=0)

    sums[...] = jnp.zeros_like(sums)
    cnt[...] = jnp.zeros_like(cnt)

    def collect(i, _):
        first = (1 - i) * 8

        @pl.when(i == 0)
        def _():
            finish(ev_in.at[pl.ds(8, 8)], ev_recv.at[1])

        @pl.when(i == 1)
        def _():
            finish(ev_in.at[pl.ds(1, 7)], ev_recv.at[0])

        tail_in = ev_in[pl.ds(first, 8), CAP:PACK, :].reshape(8 * HALF, 128)
        for part in range(2):
            main = ev_in[pl.ds(first, 8), part * HALF : (part + 1) * HALF, :]
            main = main.reshape(8 * HALF, 128)
            raw = dot(jnp.concatenate([main, tail_in], axis=1), w_both[part])
            message = (raw * sigmoid(raw)).astype(BF16)
            column = ones_where(iota((16, 128), 1) == 64 * part + TAIL)
            marks = dot_nt(column, tail_in)[0:1, :]
            here = (iota((CELLS, 8 * HALF), 0) + 1).astype(F32) == marks
            sums[...] += dot(ones_where(here), message)
            cnt[...] += jnp.sum(jnp.where(here, 1.0, 0.0), axis=1, keepdims=True)
        return 0

    lax.fori_loop(0, 2, collect, 0)
    mean_msg[...] = (sums[...] / jnp.maximum(cnt[:, 0:1], 1.0)).astype(BF16)
    loads[1].wait()

    def update(tile, _):
        def columns(gate):
            return pl.ds(pl.multiple_of(gate * WIDTH + tile * TILE, TILE), TILE)

        mean = mean_msg[...]
        gate_z = sigmoid(dot(mean, win[:, columns(0)]) + gh[:, columns(0)])
        gate_r = sigmoid(dot(mean, win[:, columns(1)]) + gh[:, columns(1)])
        cand = jnp.tanh(dot(mean, win[:, columns(2)]) + gate_r * gh[:, columns(2)])
        old = mem_ref[:, columns(0)].astype(F32)
        updated = (1.0 - gate_z) * old + gate_z * cand
        new_memory = jnp.where(cnt[:, 0:1] > 0, updated, old).astype(BF16)
        blocks[0, :, columns(0)] = new_memory
        new_ref[:, columns(0)] = new_memory
        return 0

    lax.fori_loop(0, WIDTH // TILE, update, 0)

    def bl_copy(number):
        source, target, first, rows, (dy, dx) = MESSAGES[number]
        return pltpu.make_async_remote_copy(
            src_ref=blocks.at[source, pl.ds(first, rows)],
            dst_ref=blocks.at[target, pl.ds(first, rows)],
            send_sem=bl_send.at[0],
            recv_sem=bl_recv.at[GROUP_OF[number]],
            device_id=(group, owner(dy, dx)),
            device_id_type=MESH,
        )

    def pk_copy(side, s):
        source, first, target = ((to_right, 0, right), (to_left, 2 * ROWS, left))[side]
        return pltpu.make_async_remote_copy(
            src_ref=source.at[s],
            dst_ref=picks.at[s, pl.ds(first, ROWS)],
            send_sem=pk_send.at[side],
            recv_sem=pk_recv.at[s // 2],
            device_id=(target, dev),
            device_id_type=MESH,
        )

    def arrived(awaited):
        rows = sum(MESSAGES[number][3] for number in awaited)
        if rows > CELLS:
            part = blocks.at[pl.ds(0, rows // CELLS)]
        else:
            part = blocks.at[0, pl.ds(0, rows)]
        finish(part, bl_recv.at[GROUP_OF[awaited[0]]])

    for number in START:
        bl_copy(number).start()
    loads[2].wait()
    q_ref[...] = (dot(blocks[0], wq[...]) * (HEAD**-0.5)).astype(BF16)

    for ask in asks:
        ask.wait_recv()

    def requested(s, _):
        row_hot[s, 0:ROWS, :] = chosen(reqs.at[1], s * ROLES)
        row_hot[s, ROWS : 2 * ROWS, :] = chosen(reqs.at[0], s * ROLES + 2)
        return 0

    lax.fori_loop(0, OWNERS, requested, 0)
    loads[3].wait()

    head_rows = ones_where(iota((16, WIDTH), 0) == iota((16, WIDTH), 1) // HEAD)

    def step(s, _):
        @pl.when(s < OWNERS)
        def _():
            for at, stages in STEPS.items():

                @pl.when(s == at)
                def _(stages=stages):
                    for awaited, sent in stages:
                        arrived(awaited)
                        for number in sent:
                            bl_copy(number).start()

            got = dot(row_hot[s], blocks[s]).astype(BF16)
            to_right[s] = got[0:ROWS]
            pk_copy(0, s).start()
            to_left[s] = got[ROWS : 2 * ROWS]
            pk_copy(1, s).start()
            picks[s, ROWS : 2 * ROWS, :] = got[2 * ROWS : 3 * ROWS]

        @pl.when(jnp.logical_and(s >= LAG, s % 2 == 1))
        def _():
            t = s - LAG
            finish(to_left.at[pl.ds(0, 4)], pk_recv.at[t // 2])
            picked = picks[pl.ds(t, 2)].reshape(2 * ROLES * ROWS, WIDTH)
            keys = dot(picked, wkv[:, 0:WIDTH]).astype(BF16).astype(F32)
            owned = cell_hot[pl.ds(t, 2)].reshape(2 * ROLES * ROWS, CELLS)
            product = dot(owned, q_ref[...]) * keys
            upper_part = product.astype(BF16)
            lower_part = (product - upper_part.astype(F32)).astype(BF16)
            for r in range(2 * ROLES):
                rows = slice(r * ROWS, (r + 1) * ROWS)
                score = dot_nt(head_rows, upper_part[rows]) + dot_nt(head_rows, lower_part[rows])
                first = pl.multiple_of((t * ROLES + r) * HEADS, HEADS)
                scores[pl.ds(first, HEADS), 0:ROWS] = score[0:HEADS]
            values = dot(picked, wkv[:, WIDTH:]).astype(BF16)
            for r in range(2 * ROLES):
                vals[t + r // ROLES, (r % ROLES) * LANES : (r % ROLES) * LANES + ROWS, :] = values[
                    r * ROWS : (r + 1) * ROWS
                ]

        return 0

    lax.fori_loop(0, OWNERS + LAG - 1, step, 0)

    all_scores = scores[...]
    upper_part = all_scores.astype(BF16)
    lower_part = (all_scores - upper_part.astype(F32)).astype(BF16)
    parts = jnp.concatenate([upper_part, lower_part], axis=1)
    numbers = lax.broadcasted_iota(I32, (BUCKETS, HEADS, CELLS), 0)

    def entries(j):
        return pl.ds(pl.multiple_of(j * CELLS, CELLS), CELLS)

    def order_by_cell(i, top):
        for j in range(BATCH):
            j = i * BATCH + j
            found = dot(parts, ind[:, entries(j)]).reshape(BUCKETS, HEADS, CELLS)
            inside = numbers == bkt[pl.ds(j, 1), :].reshape(1, 1, CELLS)
            mine = jnp.sum(jnp.where(inside, found, 0.0), axis=0)
            probs[j] = mine
            top = jnp.maximum(top, mine)
        return top

    lowest = jnp.full((HEADS, CELLS), -jnp.inf, F32)
    top = lax.fori_loop(0, NBR // BATCH, order_by_cell, lowest)
    raised = jnp.exp(probs[...] - top[None])
    probs[...] = (raised * (1.0 / jnp.sum(raised, axis=0))[None]).astype(BF16).astype(F32)
    scores[...] = jnp.zeros_like(scores)

    def order_by_bucket(i, _):
        placed = []
        for j in range(BATCH):
            j = i * BATCH + j
            inside = numbers == bkt[pl.ds(j, 1), :].reshape(1, 1, CELLS)
            one = jnp.where(inside, probs[j][None], 0.0).reshape(BUCKETS * HEADS, CELLS)
            placed.append(one.astype(BF16))
        part = pl.ds(pl.multiple_of(i * BATCH * CELLS, BATCH * CELLS), BATCH * CELLS)
        scores[...] += dot_nt(jnp.concatenate(placed, axis=1), ind[0:LANES, part])
        return 0

    lax.fori_loop(0, NBR // BATCH, order_by_bucket, 0)

    sums[...] = jnp.zeros_like(sums)
    widen = ones_where(iota((HEADS, WIDTH), 0) == iota((HEADS, WIDTH), 1) // HEAD)

    def weigh(i, _):
        weighted = []
        for r in range(2 * ROLES):
            first = pl.multiple_of((2 * i * ROLES + r) * HEADS, HEADS)
            wide = dot_tn(scores[pl.ds(first, HEADS), :].astype(BF16), widen)
            value = vals[2 * i + r // ROLES, (r % ROLES) * LANES : (r % ROLES + 1) * LANES, :]
            weighted.append((wide * value.astype(F32)).astype(BF16))
        cells = jnp.concatenate([cmat[2 * i], cmat[2 * i + 1]], axis=1)
        sums[...] += dot(cells, jnp.concatenate(weighted, axis=0))
        return 0

    lax.fori_loop(0, OWNERS // 2, weigh, 0)
    attended = sums[...].astype(BF16)
    loads[4].wait()
    emb_ref[...] = (blocks[0].astype(F32) + dot(attended, wout[...])).astype(BF16)

    finish(ev_out.at[pl.ds(1, OWNERS - 1)], ev_send.at[0])
    for ask in asks:
        ask.wait_send()
    finish(blocks.at[pl.ds(0, SENT_BLOCKS)], bl_send.at[0])
    finish(to_right, pk_send.at[0])
    finish(to_left, pk_send.at[1])


def body(memory, features, dest, slot, neighbours, w_message, w_input, w_hidden, w_query, w_keyval, w_output):
    inside = pl.BlockSpec(memory_space=pltpu.VMEM)
    outside = pl.BlockSpec(memory_space=pl.ANY)
    vmem, dma = pltpu.VMEM, pltpu.SemaphoreType.DMA
    return pl.pallas_call(
        kernel,
        out_shape=(
            jax.ShapeDtypeStruct((CELLS, WIDTH), BF16),
            jax.ShapeDtypeStruct((CELLS, WIDTH), BF16),
        ),
        in_specs=[inside] * 6 + [outside] * 5,
        out_specs=(inside, inside),
        scratch_shapes=[
            vmem((WIDTH, 3 * WIDTH), BF16),
            vmem((WIDTH, 3 * WIDTH), BF16),
            vmem((WIDTH, WIDTH), BF16),
            vmem((WIDTH, 2 * WIDTH), BF16),
            vmem((WIDTH, WIDTH), BF16),
            vmem((64, EVENTS), F32),
            vmem((64, WIDTH), F32),
            vmem((OWNERS, PACK, 128), BF16),
            vmem((OWNERS, PACK, 128), BF16),
            vmem((CELLS, 3 * WIDTH), F32),
            vmem((CELLS, WIDTH), F32),
            vmem((CELLS, LANES), F32),
            vmem((CELLS, WIDTH), BF16),
            vmem((2, 256, WIDTH), BF16),
            vmem((OWNERS, ROLES * ROWS, CELLS), BF16),
            vmem((OWNERS, ROLES * ROWS, CELLS), BF16),
            vmem((NBR, CELLS), I32),
            vmem((NBR, CELLS), I32),
            vmem((LANES, LANES), F32),
            vmem((2 * LANES, NBR * CELLS), BF16),
            vmem((LANES, LANES), BF16),
            vmem((2, LANES, LANES), BF16),
            vmem((BUCKETS, LANES), F32),
            vmem((OWNERS, CELLS, ROLES * LANES), BF16),
            vmem((OWNERS, CELLS, WIDTH), BF16),
            vmem((OWNERS, ROLES * ROWS, WIDTH), BF16),
            vmem((OWNERS, ROWS, WIDTH), BF16),
            vmem((OWNERS, ROWS, WIDTH), BF16),
            vmem((CELLS, WIDTH), BF16),
            vmem((OWNERS, ROLES * LANES, WIDTH), BF16),
            vmem((BUCKETS * HEADS, LANES), F32),
            vmem((NBR, HEADS, CELLS), F32),
            dma((5,)),
            dma((1,)),
            dma((2,)),
            dma((2,)),
            dma((2,)),
            dma((1,)),
            dma((len(GROUPS),)),
            dma((2,)),
            dma((OWNERS // 2,)),
        ],
        compiler_params=pltpu.CompilerParams(
            collective_id=0, has_side_effects=True, vmem_limit_bytes=58 * 1024 * 1024
        ),
        cost_estimate=pl.CostEstimate(
            flops=12_000_000_000, bytes_accessed=6_000_000, transcendentals=2_000_000
        ),
    )(
        memory,
        features.T,
        dest.reshape(1, EVENTS),
        slot.reshape(1, EVENTS),
        neighbours.T,
        w_message,
        w_input,
        w_hidden,
        w_query,
        w_keyval,
        w_output,
    )


def solution(mesh):
    rows = P(("group", "dev"), None)
    placed = (rows, rows, rows, P(("group", "dev")), rows) + (P(),) * 6
    return jax.shard_map(
        body, mesh=mesh, in_specs=placed, out_specs=(rows, rows), check_vma=False
    )
```

```python
import jax
import jax.numpy as jnp
from jax import lax
from jax.experimental import pallas as pl
from jax.experimental.pallas import tpu as pltpu
from jax.sharding import PartitionSpec as P

MESH = pl.DeviceIdType.MESH
F32, BF16, I32 = jnp.float32, jnp.bfloat16, jnp.int32

HEADS = 8
HEAD = 64
NBR = 20
CELLS = 256
WIDTH = 512
EVENTS = 512
CAP = 96
HALF = CAP // 2
PACK = CAP + HALF
FEAT = 172
TAIL = FEAT - 128
ROWS = 112
LANES = 128
ROLES = 3
OWNERS = 16
SIDE = 4
RANGES = 16
BUCKETS = OWNERS * ROLES
TILE = 256
LAG = 7
EARLY = ((16, 0, 10),)
LAST = (10, 16)
LOWEST = -3.0e38
BATCH = 4

ORDER = (
    (0, 0), (0, 3), (0, 1), (3, 0), (1, 0), (3, 3), (1, 1), (0, 2),
    (2, 0), (3, 1), (1, 3), (3, 2), (1, 2), (2, 3), (2, 1), (2, 2),
)
SLOT = {rel: slot for slot, rel in enumerate(ORDER)}


def gather_plan():
    names, messages = {}, []

    def add(name, source, hop, first, rows):
        target = ((source[0] - hop[0]) % SIDE, (source[1] - hop[1]) % SIDE)
        names[name] = len(messages)
        messages.append((SLOT[source], SLOT[target], first, rows, hop))

    for cls in "ab":
        base = 0 if cls == "a" else 128

        def at(first, second, cls=cls):
            return (second % SIDE, first % SIDE) if cls == "a" else (first % SIDE, second % SIDE)

        for sign in (1, -1):
            add((cls, 1, 0, sign), at(0, 0), at(sign, 0), base, 128)
            add((cls, 2, 0, sign), at(-sign, 0), at(sign, 0), base + (0 if sign > 0 else 64), 64)
            for off in (0, -1, 1, 2):
                add((cls, 3, off, sign), at(off, 0), at(0, sign), base, 128)
                first = base + (0 if sign > 0 else 64)
                add((cls, 4, off, sign), at(off, -sign), at(0, sign), first, 64)

    def both(*items):
        return [names[(cls,) + item] for item in items for cls in "ab"]

    start = both((1, 0, 1), (1, 0, -1), (3, 0, 1), (3, 0, -1))
    steps = {
        1: [
            (
                both((1, 0, 1), (1, 0, -1)),
                both((2, 0, 1), (2, 0, -1), (3, -1, 1), (3, 1, -1)),
            ),
            (
                both((3, 0, 1), (3, 0, -1)),
                both((4, 0, 1), (4, 0, -1), (3, 1, 1), (3, -1, -1)),
            ),
        ],
        3: [(both((2, 0, 1), (2, 0, -1)), both((3, 2, 1), (3, 2, -1)))],
        5: [(both((3, -1, 1)), both((4, -1, 1)))],
        6: [(both((3, 1, -1)), both((4, 1, -1)))],
        7: [([names[("b", 4, 0, 1)], names[("b", 4, 0, -1)]], [])],
        8: [([names[("a", 4, 0, 1)], names[("a", 4, 0, -1)]], [])],
        9: [
            (
                [names[("a", 3, 1, 1)], names[("b", 3, -1, -1)]],
                [names[("a", 4, 1, 1)], names[("b", 4, -1, -1)]],
            )
        ],
        10: [
            (
                [names[("a", 3, -1, -1)], names[("b", 3, 1, 1)]],
                [names[("a", 4, -1, -1)], names[("b", 4, 1, 1)]],
            )
        ],
        11: [
            (both((3, 2, 1), (3, 2, -1)), both((4, 2, 1), (4, 2, -1))),
            ([names[("b", 4, -1, 1)], names[("b", 4, -1, -1)]], []),
        ],
        12: [([names[("b", 4, 1, 1)], names[("b", 4, 1, -1)]], [])],
        13: [([names[("a", 4, -1, 1)], names[("a", 4, -1, -1)]], [])],
        14: [([names[("a", 4, 1, 1)], names[("a", 4, 1, -1)]], [])],
        15: [(both((4, 2, 1), (4, 2, -1)), [])],
    }
    return messages, start, steps


MESSAGES, START, STEPS = gather_plan()
COUNT = len(MESSAGES)
GROUPS = [awaited for stages in STEPS.values() for awaited, _ in stages]
GROUP_OF = {number: group for group, awaited in enumerate(GROUPS) for number in awaited}
SENT_BLOCKS = sum(message[3] for message in MESSAGES) // CELLS


def iota(shape, dim):
    return lax.broadcasted_iota(I32, shape, dim)


def dot(a, b):
    return jnp.dot(a, b, preferred_element_type=F32)


def dot_nt(a, b):
    return lax.dot_general(a, b, (((1,), (1,)), ((), ())), preferred_element_type=F32)


def dot_tn(a, b):
    return lax.dot_general(a, b, (((0,), (0,)), ((), ())), preferred_element_type=F32)


def ones_where(mask):
    return jnp.where(mask, 1.0, 0.0).astype(BF16)


def sigmoid(x):
    return 0.5 * jnp.tanh(0.5 * x) + 0.5


def kernel(
    mem_hbm, feat_hbm, dest_hbm, slot_hbm, nbr_hbm, wmsg_hbm, win_hbm, whid_hbm, wq_hbm, wkv_hbm,
    new_ref, att_ref,
    mem_ref, feat_ref, dest_ref, slot_ref, nbr_ref, wmsg_ref, win, whid, wqkv, order,
    tail, wtail, ev_out, ev_in, gh, sums, cnt,
    mean_msg, w_both, row_hot, cell_hot, bkt, wanted, table, ind, tabs, reqs, celltab, cmat,
    stats, blocks, picks, to_left, to_right, q_ref, vals, scores, probs, widen_all,
    w_sem, ev_send, ev_recv, rq_send, rq_recv, bl_send, bl_recv, pk_send, pk_recv,
):
    group, dev = lax.axis_index("group"), lax.axis_index("dev")
    y, x = dev // SIDE, dev % SIDE
    left, right = (group + RANGES - 1) % RANGES, (group + 1) % RANGES

    def owner(dy, dx):
        return ((y + dy) % SIDE) * SIDE + (x + dx) % SIDE

    def finish(part, sem):
        pltpu.make_async_copy(part, part, sem).wait()

    barrier = pltpu.get_barrier_semaphore()

    for side in (left, right):
        pl.semaphore_signal(barrier, inc=1, device_id=(side, dev), device_id_type=MESH)

    def greet(k, _):
        pl.semaphore_signal(
            barrier, inc=1, device_id=(group, owner(k // SIDE, k % SIDE)), device_id_type=MESH
        )
        return 0

    lax.fori_loop(1, OWNERS, greet, 0)

    loads = [
        pltpu.make_async_copy(src, dst, w_sem.at[i])
        for i, (src, dst) in enumerate(
            (
                (whid_hbm, whid),
                (win_hbm, win),
                (wq_hbm, wqkv.at[0]),
                (wkv_hbm.at[:, pl.ds(0, WIDTH)], wqkv.at[1]),
                (wkv_hbm.at[:, pl.ds(WIDTH, WIDTH)], wqkv.at[2]),
                (feat_hbm, feat_ref),
                (dest_hbm, dest_ref),
                (slot_hbm, slot_ref),
                (nbr_hbm, nbr_ref),
                (mem_hbm, mem_ref),
                (wmsg_hbm, wmsg_ref),
            )
        )
    ]
    for load in loads[5:] + loads[:5]:
        load.start()
    for load in loads[5:8]:
        load.wait()

    tail[...] = jnp.zeros_like(tail)
    tail[0:TAIL, :] = feat_ref[128:FEAT, :].astype(F32)
    tail[TAIL : TAIL + 1, :] = (slot_ref[...] + 1).astype(F32)
    tails = tail[...].astype(BF16)
    blank = jnp.zeros((64, EVENTS), BF16)
    head = feat_ref[0:128, :]
    feats = (
        jnp.concatenate([head, tails, blank], axis=0),
        jnp.concatenate([head, blank, tails], axis=0),
    )
    dest = dest_ref[...]
    mine = iota((OWNERS, EVENTS), 0) == dest
    upper = ones_where(iota((EVENTS, EVENTS), 0) < iota((EVENTS, EVENTS), 1))
    before = dot(ones_where(mine), upper)
    place = jnp.sum(jnp.where(mine, before, 0.0), axis=0, keepdims=True).astype(I32) + dest * CAP

    def ev_copy(k):
        return pltpu.make_async_remote_copy(
            src_ref=ev_out.at[k],
            dst_ref=ev_in.at[k],
            send_sem=ev_send.at[0],
            recv_sem=ev_recv.at[k // 8],
            device_id=(group, owner(k // SIDE, k % SIDE)),
            device_id_type=MESH,
        )

    def pack(i, _):
        rows = SIDE - 1 - i
        packed = []
        for part in range(2):
            pick = [
                iota((HALF, EVENTS), 0) == place - (owner(rows, column) * CAP + part * HALF)
                for column in range(SIDE)
            ]
            pick = jnp.concatenate([ones_where(one) for one in pick], axis=0)
            packed.append(dot_nt(pick, feats[part]))
        for column in range(SIDE):
            k = rows * SIDE + column
            at = slice(column * HALF, (column + 1) * HALF)
            ev_out[k, 0:HALF, :] = packed[0][at, 0:128].astype(BF16)
            ev_out[k, HALF:CAP, :] = packed[1][at, 0:128].astype(BF16)
            ev_out[k, CAP:PACK, :] = (packed[0][at, 128:] + packed[1][at, 128:]).astype(BF16)
        return 0

    lax.fori_loop(0, SIDE, pack, 0)
    ev_in[0] = ev_out[0]
    pl.semaphore_wait(barrier, OWNERS - 1 + 2)

    def send_events(i, _):
        ev_copy(OWNERS - 1 - i).start()
        return 0

    lax.fori_loop(0, OWNERS - 1, send_events, 0)

    loads[8].wait()
    ids = nbr_ref[...]
    role = ((ids >> 12) - group + 1 + RANGES) % RANGES
    named = (ids >> 8) & 15
    rel = (((named >> 2) - y) & 3) * SIDE + ((named - x) & 3)
    slot_of = jnp.zeros_like(rel)
    for number, (dy, dx) in enumerate(ORDER):
        slot_of = jnp.where(rel == dy * SIDE + dx, number, slot_of)
    bucket = slot_of * ROLES + role
    bkt[...] = bucket
    wanted[...] = (ids & 255) + 1
    ahead = ones_where(iota((CELLS, CELLS), 0) < iota((CELLS, CELLS), 1))
    bucket_ids, place_ids = iota((BUCKETS, CELLS), 0), iota((LANES, CELLS), 0)
    cell = jnp.broadcast_to((iota((1, CELLS), 1) + 1).astype(F32), (BUCKETS, CELLS))
    filler = jnp.zeros((LANES - 2 * BUCKETS, CELLS), BF16)
    table[...] = jnp.zeros_like(table)

    def tabulate(i, offset):
        inside = [bucket_ids == bkt[pl.ds(i * BATCH + j, 1), :] for j in range(BATCH)]
        before = dot(jnp.concatenate([ones_where(one) for one in inside], axis=0), ahead)
        hots, boths = [], []
        for j in range(BATCH):
            rank = before[j * BUCKETS : (j + 1) * BUCKETS] + offset
            offset = offset + jnp.sum(jnp.where(inside[j], 1.0, 0.0), axis=1, keepdims=True)
            rank = jnp.sum(jnp.where(inside[j], rank, 0.0), axis=0, keepdims=True).astype(I32)
            hot = ones_where(place_ids == rank)
            at = pl.ds(pl.multiple_of((i * BATCH + j) * CELLS, CELLS), CELLS)
            ind[0:LANES, at] = hot
            ind[LANES : 2 * LANES, at] = hot
            row = wanted[pl.ds(i * BATCH + j, 1), :].astype(F32)
            asked = jnp.where(inside[j], row, 0.0).astype(BF16)
            by = jnp.where(inside[j], cell, 0.0).astype(BF16)
            hots.append(hot)
            boths.append(jnp.concatenate([asked, by, filler], axis=0))
        table[...] += dot_nt(jnp.concatenate(hots, axis=1), jnp.concatenate(boths, axis=1))
        return offset

    lax.fori_loop(0, NBR // BATCH, tabulate, jnp.zeros((BUCKETS, 1), F32))
    tabs[...] = table[...].astype(BF16)
    celltab[...] = table[...].T[BUCKETS : 2 * BUCKETS, :]

    asks = [
        pltpu.make_async_remote_copy(
            src_ref=tabs,
            dst_ref=reqs.at[i],
            send_sem=rq_send.at[i],
            recv_sem=rq_recv.at[i],
            device_id=(side, dev),
            device_id_type=MESH,
        )
        for i, side in enumerate((right, left))
    ]
    for ask in asks:
        ask.start()

    every = jnp.ones((LANES, CELLS), BF16)

    def chosen(*wanted):
        lane = iota((ROWS, LANES), 1)
        columns = [
            jnp.where(lane == column, tab[0:ROWS, :].astype(F32), 0.0).astype(BF16)
            for tab, column in wanted
        ]
        rows = ROWS * len(columns)
        values = dot(jnp.concatenate(columns, axis=0), every)
        return ones_where(values == (iota((rows, CELLS), 1) + 1).astype(F32))

    def own_tables(i, _):
        for s in (2 * i, 2 * i + 1):
            first = s * ROLES
            hot = chosen(
                (tabs, BUCKETS + first),
                (tabs, BUCKETS + first + 1),
                (tabs, BUCKETS + first + 2),
                (tabs, first + 1),
            )
            cell_hot[s] = hot[0 : ROLES * ROWS]
            row_hot[s, 2 * ROWS : 3 * ROWS, :] = hot[ROLES * ROWS :]
        return 0

    lax.fori_loop(0, OWNERS // 2, own_tables, 0)
    loads[9].wait()
    loads[10].wait()
    loads[0].wait()

    def hidden(part, _):
        columns = pl.ds(pl.multiple_of(part * WIDTH, WIDTH), WIDTH)
        gh[:, columns] = dot(mem_ref[...], whid[:, columns])
        return 0

    lax.fori_loop(0, 3, hidden, 0)

    column = iota((1, WIDTH), 1)
    order[...] = ones_where(
        iota((WIDTH, WIDTH), 0) == (column % HEADS) * HEAD + column // HEADS
    )
    for load in loads[2:5]:
        load.wait()

    def reorder(part, _):
        wqkv[part] = dot(wqkv[part], order[...]).astype(BF16)
        return 0

    lax.fori_loop(0, 3, reorder, 0)

    wtail[...] = jnp.zeros_like(wtail)
    wtail[0:TAIL, :] = wmsg_ref[128:FEAT, :].astype(F32)
    w_tail = wtail[...].astype(BF16)
    w_blank = jnp.zeros((64, WIDTH), BF16)
    w_both[0] = jnp.concatenate([wmsg_ref[0:128, :], w_tail, w_blank], axis=0)
    w_both[1] = jnp.concatenate([wmsg_ref[0:128, :], w_blank, w_tail], axis=0)

    sums[...] = jnp.zeros_like(sums)
    cnt[...] = jnp.zeros_like(cnt)

    def collect(i, _):
        first = (1 - i) * 8

        @pl.when(i == 0)
        def _():
            finish(ev_in.at[pl.ds(8, 8)], ev_recv.at[1])

        @pl.when(i == 1)
        def _():
            finish(ev_in.at[pl.ds(1, 7)], ev_recv.at[0])

        tail_in = ev_in[pl.ds(first, 8), CAP:PACK, :].reshape(8 * HALF, 128)
        for part in range(2):
            main = ev_in[pl.ds(first, 8), part * HALF : (part + 1) * HALF, :]
            main = main.reshape(8 * HALF, 128)
            raw = dot(jnp.concatenate([main, tail_in], axis=1), w_both[part])
            half = 0.5 * raw
            message = (half + half * jnp.tanh(half)).astype(BF16)
            column = ones_where(iota((16, 128), 1) == 64 * part + TAIL)
            marks = dot_nt(column, tail_in)[0:1, :]
            here = (iota((CELLS, 8 * HALF), 0) + 1).astype(F32) == marks
            sums[...] += dot(ones_where(here), message)
            cnt[...] += jnp.sum(jnp.where(here, 1.0, 0.0), axis=1, keepdims=True)
        return 0

    lax.fori_loop(0, 2, collect, 0)
    mean_msg[...] = (sums[...] / jnp.maximum(cnt[:, 0:1], 1.0)).astype(BF16)
    loads[1].wait()

    def update(tile, _):
        def columns(gate):
            return pl.ds(pl.multiple_of(gate * WIDTH + tile * TILE, TILE), TILE)

        mean = mean_msg[...]
        gate_z = sigmoid(dot(mean, win[:, columns(0)]) + gh[:, columns(0)])
        gate_r = sigmoid(dot(mean, win[:, columns(1)]) + gh[:, columns(1)])
        cand = jnp.tanh(dot(mean, win[:, columns(2)]) + gate_r * gh[:, columns(2)])
        old = mem_ref[:, columns(0)].astype(F32)
        updated = (1.0 - gate_z) * old + gate_z * cand
        new_memory = jnp.where(cnt[:, 0:1] > 0, updated, old).astype(BF16)
        blocks[0, :, columns(0)] = new_memory
        new_ref[:, columns(0)] = new_memory
        return 0

    lax.fori_loop(0, WIDTH // TILE, update, 0)

    def bl_copy(number):
        source, target, first, rows, (dy, dx) = MESSAGES[number]
        return pltpu.make_async_remote_copy(
            src_ref=blocks.at[source, pl.ds(first, rows)],
            dst_ref=blocks.at[target, pl.ds(first, rows)],
            send_sem=bl_send.at[0],
            recv_sem=bl_recv.at[GROUP_OF[number]],
            device_id=(group, owner(dy, dx)),
            device_id_type=MESH,
        )

    def pk_copy(side, s):
        source, first, target = ((to_right, 0, right), (to_left, 2 * ROWS, left))[side]
        return pltpu.make_async_remote_copy(
            src_ref=source.at[s],
            dst_ref=picks.at[s, pl.ds(first, ROWS)],
            send_sem=pk_send.at[side],
            recv_sem=pk_recv.at[(s + 1) // 2],
            device_id=(target, dev),
            device_id_type=MESH,
        )

    def arrived(awaited):
        rows = sum(MESSAGES[number][3] for number in awaited)
        if rows > CELLS:
            part = blocks.at[pl.ds(0, rows // CELLS)]
        else:
            part = blocks.at[0, pl.ds(0, rows)]
        finish(part, bl_recv.at[GROUP_OF[awaited[0]]])

    for number in START:
        bl_copy(number).start()
    q_ref[...] = (dot(blocks[0], wqkv[0]) * (HEAD**-0.5)).astype(BF16)

    for ask in asks:
        ask.wait_recv()

    def requested(i, _):
        for s in (2 * i, 2 * i + 1):
            row_hot[s, 0 : 2 * ROWS, :] = chosen(
                (reqs.at[1], s * ROLES), (reqs.at[0], s * ROLES + 2)
            )
            for r in range(ROLES):
                row = celltab[pl.ds(s * ROLES + r, 1), :]
                hot = ones_where((iota((CELLS, LANES), 0) + 1).astype(F32) == row)
                cmat[s, :, r * LANES : (r + 1) * LANES] = hot
                vals[s, r * LANES + ROWS : (r + 1) * LANES, :] = blank_rows
        return 0

    blank_rows = jnp.zeros((LANES - ROWS, WIDTH), BF16)
    lax.fori_loop(0, OWNERS // 2, requested, 0)

    head_rows = ones_where(iota((16, 2 * LANES), 1) % HEADS == iota((16, 2 * LANES), 0))

    widen = ones_where(iota((HEADS, WIDTH), 0) == iota((HEADS, WIDTH), 1) % HEADS)
    group_heads = 2 * ROLES * HEADS
    lane = iota((group_heads, 2 * ROLES * LANES), 1)
    head_of = lane // LANES * HEADS + lane % HEADS
    widen_all[...] = ones_where(iota((group_heads, 2 * ROLES * LANES), 0) == head_of)

    def entries(j):
        return pl.ds(pl.multiple_of(j * CELLS, CELLS), CELLS)

    def attend(begin, end):
        low, high = begin * ROLES, end * ROLES
        rows = slice(low * HEADS, high * HEADS)
        part = scores[rows, :]
        upper_part = part.astype(BF16)
        lower_part = (part - upper_part.astype(F32)).astype(BF16)
        parts = jnp.concatenate([upper_part, lower_part], axis=1)
        numbers = lax.broadcasted_iota(I32, (high - low, HEADS, CELLS), 0) + low

        def order_by_cell(i, top):
            for j in range(BATCH):
                j = i * BATCH + j
                found = dot(parts, ind[:, entries(j)]).reshape(high - low, HEADS, CELLS)
                bucket = bkt[pl.ds(j, 1), :]
                inside = numbers == bucket.reshape(1, 1, CELLS)
                mine = jnp.sum(jnp.where(inside, found, 0.0), axis=0)
                mine = jnp.where(jnp.logical_and(bucket >= low, bucket < high), mine, LOWEST)
                probs[j] = mine
                top = jnp.maximum(top, mine)
            return top

        lowest = jnp.full((HEADS, CELLS), LOWEST, F32)
        top = lax.fori_loop(0, NBR // BATCH, order_by_cell, lowest)
        if begin > 0:
            top = jnp.maximum(top, stats[0])
        found = probs[...]
        raised = jnp.where(found == LOWEST, 0.0, jnp.exp(found - top[None]))
        total = jnp.sum(raised, axis=0)
        if begin > 0:
            scale = jnp.exp(stats[0] - top)
            total = total + stats[1] * scale
            if end == OWNERS:
                inverse = 1.0 / total
                raised = raised * inverse[None]
                scale = scale * inverse
            upper_part = scale.astype(BF16)
            lower_part = (scale - upper_part.astype(F32)).astype(BF16)
            sums[...] = sums[...] * (dot_tn(upper_part, widen) + dot_tn(lower_part, widen))
        else:
            sums[...] = jnp.zeros_like(sums)
        stats[0] = top
        stats[1] = total
        probs[...] = raised
        scores[rows, :] = jnp.zeros_like(part)

        def order_by_bucket(i, _):
            placed = []
            for j in range(BATCH):
                j = i * BATCH + j
                inside = numbers == bkt[pl.ds(j, 1), :].reshape(1, 1, CELLS)
                one = jnp.where(inside, probs[j][None], 0.0)
                placed.append(one.reshape((high - low) * HEADS, CELLS).astype(BF16))
            part = pl.ds(pl.multiple_of(i * BATCH * CELLS, BATCH * CELLS), BATCH * CELLS)
            scores[rows, :] += dot_nt(jnp.concatenate(placed, axis=1), ind[0:LANES, part])
            return 0

        lax.fori_loop(0, NBR // BATCH, order_by_bucket, 0)

        def weigh(i, _):
            weighted = []
            first = pl.multiple_of(i * group_heads, group_heads)
            weights = scores[pl.ds(first, group_heads), :].T.astype(BF16)
            wide = dot(weights, widen_all[...]).astype(BF16)
            for r in range(2 * ROLES):
                value = vals[2 * i + r // ROLES, (r % ROLES) * LANES : (r % ROLES + 1) * LANES, :]
                weight = wide[:, r * LANES : (r + 1) * LANES]
                weight = jnp.concatenate([weight] * (WIDTH // LANES), axis=1)
                weighted.append(weight * value)
            cells = jnp.concatenate([cmat[2 * i], cmat[2 * i + 1]], axis=1)
            sums[...] += dot(cells, jnp.concatenate(weighted, axis=0))
            return 0

        lax.fori_loop(begin // 2, end // 2, weigh, 0)

    def pick_rows(s):
        got = dot(row_hot[s], blocks[s]).astype(BF16)
        to_right[s] = got[0:ROWS]
        pk_copy(0, s).start()
        to_left[s] = got[ROWS : 2 * ROWS]
        pk_copy(1, s).start()
        picks[s, ROWS : 2 * ROWS, :] = got[2 * ROWS : 3 * ROWS]

    def score_slots(t, number):
        finish(to_left.at[pl.ds(0, 2 * number)], pk_recv.at[(t + 1) // 2])
        picked = picks[pl.ds(t, number)].reshape(number * ROLES * ROWS, WIDTH)
        owned = cell_hot[pl.ds(t, number)].reshape(number * ROLES * ROWS, CELLS)
        keys = dot(picked, wqkv[1]).astype(BF16).astype(F32)
        product = dot(owned, q_ref[...]) * keys
        tiles = [product[:, i * LANES : (i + 1) * LANES] for i in range(WIDTH // LANES)]
        product = (tiles[0] + tiles[1]) + (tiles[2] + tiles[3])
        upper_part = product.astype(BF16)
        lower_part = (product - upper_part.astype(F32)).astype(BF16)
        split = jnp.concatenate([upper_part, lower_part], axis=1)
        values = dot(picked, wqkv[2]).astype(BF16)
        for r in range(number * ROLES):
            rows = slice(r * ROWS, (r + 1) * ROWS)
            first = pl.multiple_of((t * ROLES + r) * HEADS, HEADS)
            scores[pl.ds(first, HEADS), 0:ROWS] = dot_nt(head_rows, split[rows])[0:HEADS]
            vals[t + r // ROLES, (r % ROLES) * LANES : (r % ROLES) * LANES + ROWS, :] = values[rows]

    def step(s, _):
        @pl.when(s < OWNERS)
        def _():
            for at, stages in STEPS.items():

                @pl.when(s == at)
                def _(stages=stages):
                    for awaited, sent in stages:
                        arrived(awaited)
                        for number in sent:
                            bl_copy(number).start()

            pick_rows(s)

        for after, begin, end in EARLY:

            @pl.when(s == after)
            def _(begin=begin, end=end):
                attend(begin, end)

        @pl.when(jnp.logical_and(jnp.logical_and(s >= LAG, s < OWNERS + LAG - 2), s % 2 == 1))
        def _():
            score_slots(s - LAG + 1, 2)

        @pl.when(jnp.logical_or(s == LAG - 1, s == OWNERS + LAG - 2))
        def _():
            score_slots((s // OWNERS) * (OWNERS - 1), 1)

        return 0

    lax.fori_loop(0, OWNERS + LAG - 1, step, 0)

    attend(*LAST)
    att_ref[...] = dot_nt(sums[...].astype(BF16), order[...]).astype(BF16)

    finish(ev_out.at[pl.ds(1, OWNERS - 1)], ev_send.at[0])
    for ask in asks:
        ask.wait_send()
    finish(blocks.at[pl.ds(0, SENT_BLOCKS)], bl_send.at[0])
    finish(to_right, pk_send.at[0])
    finish(to_left, pk_send.at[1])


def embed(new_in, att_ref, wout_ref, new_ref, emb_ref):
    new_memory = new_in[...]
    new_ref[...] = new_memory
    emb_ref[...] = (new_memory.astype(F32) + dot(att_ref[...], wout_ref[...])).astype(BF16)


def body(memory, features, dest, slot, neighbours, w_message, w_input, w_hidden, w_query, w_keyval, w_output):
    inside = pl.BlockSpec(memory_space=pltpu.VMEM)
    outside = pl.BlockSpec(memory_space=pl.ANY)
    vmem, dma = pltpu.VMEM, pltpu.SemaphoreType.DMA
    new_memory, attended = pl.pallas_call(
        kernel,
        out_shape=(
            jax.ShapeDtypeStruct((CELLS, WIDTH), BF16),
            jax.ShapeDtypeStruct((CELLS, WIDTH), BF16),
        ),
        in_specs=[outside] * 10,
        out_specs=(inside, inside),
        scratch_shapes=[
            vmem((CELLS, WIDTH), BF16),
            vmem((FEAT, EVENTS), BF16),
            vmem((1, EVENTS), I32),
            vmem((1, EVENTS), I32),
            vmem((NBR, CELLS), I32),
            vmem((FEAT, WIDTH), BF16),
            vmem((WIDTH, 3 * WIDTH), BF16),
            vmem((WIDTH, 3 * WIDTH), BF16),
            vmem((3, WIDTH, WIDTH), BF16),
            vmem((WIDTH, WIDTH), BF16),
            vmem((64, EVENTS), F32),
            vmem((64, WIDTH), F32),
            vmem((OWNERS, PACK, 128), BF16),
            vmem((OWNERS, PACK, 128), BF16),
            vmem((CELLS, 3 * WIDTH), F32),
            vmem((CELLS, WIDTH), F32),
            vmem((CELLS, LANES), F32),
            vmem((CELLS, WIDTH), BF16),
            vmem((2, 256, WIDTH), BF16),
            vmem((OWNERS, ROLES * ROWS, CELLS), BF16),
            vmem((OWNERS, ROLES * ROWS, CELLS), BF16),
            vmem((NBR, CELLS), I32),
            vmem((NBR, CELLS), I32),
            vmem((LANES, LANES), F32),
            vmem((2 * LANES, NBR * CELLS), BF16),
            vmem((LANES, LANES), BF16),
            vmem((2, LANES, LANES), BF16),
            vmem((BUCKETS, LANES), F32),
            vmem((OWNERS, CELLS, ROLES * LANES), BF16),
            vmem((2, HEADS, CELLS), F32),
            vmem((OWNERS, CELLS, WIDTH), BF16),
            vmem((OWNERS, ROLES * ROWS, WIDTH), BF16),
            vmem((OWNERS, ROWS, WIDTH), BF16),
            vmem((OWNERS, ROWS, WIDTH), BF16),
            vmem((CELLS, WIDTH), BF16),
            vmem((OWNERS, ROLES * LANES, WIDTH), BF16),
            vmem((BUCKETS * HEADS, LANES), F32),
            vmem((NBR, HEADS, CELLS), F32),
            vmem((2 * ROLES * HEADS, 2 * ROLES * LANES), BF16),
            dma((11,)),
            dma((1,)),
            dma((2,)),
            dma((2,)),
            dma((2,)),
            dma((1,)),
            dma((len(GROUPS),)),
            dma((2,)),
            dma((OWNERS // 2 + 1,)),
        ],
        compiler_params=pltpu.CompilerParams(
            collective_id=0, has_side_effects=True, vmem_limit_bytes=58 * 1024 * 1024
        ),
        cost_estimate=pl.CostEstimate(
            flops=12_000_000_000, bytes_accessed=6_000_000, transcendentals=2_000_000
        ),
    )(
        memory,
        features.T,
        dest.reshape(1, EVENTS),
        slot.reshape(1, EVENTS),
        neighbours.T,
        w_message,
        w_input,
        w_hidden,
        w_query,
        w_keyval,
    )
    return pl.pallas_call(
        embed,
        out_shape=(
            jax.ShapeDtypeStruct((CELLS, WIDTH), BF16),
            jax.ShapeDtypeStruct((CELLS, WIDTH), BF16),
        ),
        in_specs=[inside] * 3,
        out_specs=(inside, inside),
    )(new_memory, attended, w_output)


def solution(mesh):
    rows = P(("group", "dev"), None)
    placed = (rows, rows, rows, P(("group", "dev")), rows) + (P(),) * 6
    return jax.shard_map(
        body, mesh=mesh, in_specs=placed, out_specs=(rows, rows), check_vma=False
    )
```

```python
import jax
import jax.numpy as jnp
from jax import lax
from jax.experimental import pallas as pl
from jax.experimental.pallas import tpu as pltpu
from jax.sharding import PartitionSpec as P

MESH = pl.DeviceIdType.MESH
F32, BF16, I32 = jnp.float32, jnp.bfloat16, jnp.int32

HEADS = 8
HEAD = 64
NBR = 20
CELLS = 256
WIDTH = 512
EVENTS = 512
CAP = 96
HALF = CAP // 2
PACK = CAP + HALF
FEAT = 172
TAIL = FEAT - 128
ROWS = 112
LANES = 128
ROLES = 3
OWNERS = 16
SIDE = 4
RANGES = 16
BUCKETS = OWNERS * ROLES
TILE = 256
LAG = 7
EARLY = ((16, 0, 10),)
LAST = (10, 16)
LOWEST = -3.0e38
BATCH = 4

ORDER = (
    (0, 0), (0, 3), (0, 1), (3, 0), (1, 0), (3, 3), (1, 1), (0, 2),
    (2, 0), (3, 1), (1, 3), (3, 2), (1, 2), (2, 3), (2, 1), (2, 2),
)
SLOT = {rel: slot for slot, rel in enumerate(ORDER)}


def gather_plan():
    names, messages = {}, []

    def add(name, source, hop, first, rows):
        target = ((source[0] - hop[0]) % SIDE, (source[1] - hop[1]) % SIDE)
        names[name] = len(messages)
        messages.append((SLOT[source], SLOT[target], first, rows, hop))

    for cls in "ab":
        base = 0 if cls == "a" else 128

        def at(first, second, cls=cls):
            return (second % SIDE, first % SIDE) if cls == "a" else (first % SIDE, second % SIDE)

        for sign in (1, -1):
            add((cls, 1, 0, sign), at(0, 0), at(sign, 0), base, 128)
            add((cls, 2, 0, sign), at(-sign, 0), at(sign, 0), base + (0 if sign > 0 else 64), 64)
            for off in (0, -1, 1, 2):
                add((cls, 3, off, sign), at(off, 0), at(0, sign), base, 128)
                first = base + (0 if sign > 0 else 64)
                add((cls, 4, off, sign), at(off, -sign), at(0, sign), first, 64)

    def both(*items):
        return [names[(cls,) + item] for item in items for cls in "ab"]

    start = both((1, 0, 1), (1, 0, -1), (3, 0, 1), (3, 0, -1))
    steps = {
        1: [
            (
                both((1, 0, 1), (1, 0, -1)),
                both((2, 0, 1), (2, 0, -1), (3, -1, 1), (3, 1, -1)),
            ),
            (
                both((3, 0, 1), (3, 0, -1)),
                both((4, 0, 1), (4, 0, -1), (3, 1, 1), (3, -1, -1)),
            ),
        ],
        3: [(both((2, 0, 1), (2, 0, -1)), both((3, 2, 1), (3, 2, -1)))],
        5: [(both((3, -1, 1)), both((4, -1, 1)))],
        6: [(both((3, 1, -1)), both((4, 1, -1)))],
        7: [([names[("b", 4, 0, 1)], names[("b", 4, 0, -1)]], [])],
        8: [([names[("a", 4, 0, 1)], names[("a", 4, 0, -1)]], [])],
        9: [
            (
                [names[("a", 3, 1, 1)], names[("b", 3, -1, -1)]],
                [names[("a", 4, 1, 1)], names[("b", 4, -1, -1)]],
            )
        ],
        10: [
            (
                [names[("a", 3, -1, -1)], names[("b", 3, 1, 1)]],
                [names[("a", 4, -1, -1)], names[("b", 4, 1, 1)]],
            )
        ],
        11: [
            (both((3, 2, 1), (3, 2, -1)), both((4, 2, 1), (4, 2, -1))),
            ([names[("b", 4, -1, 1)], names[("b", 4, -1, -1)]], []),
        ],
        12: [([names[("b", 4, 1, 1)], names[("b", 4, 1, -1)]], [])],
        13: [([names[("a", 4, -1, 1)], names[("a", 4, -1, -1)]], [])],
        14: [([names[("a", 4, 1, 1)], names[("a", 4, 1, -1)]], [])],
        15: [(both((4, 2, 1), (4, 2, -1)), [])],
    }
    return messages, start, steps


MESSAGES, START, STEPS = gather_plan()
COUNT = len(MESSAGES)
GROUPS = [awaited for stages in STEPS.values() for awaited, _ in stages]
GROUP_OF = {number: group for group, awaited in enumerate(GROUPS) for number in awaited}
SENT_BLOCKS = sum(message[3] for message in MESSAGES) // CELLS


def iota(shape, dim):
    return lax.broadcasted_iota(I32, shape, dim)


def dot(a, b):
    return jnp.dot(a, b, preferred_element_type=F32)


def dot_nt(a, b):
    return lax.dot_general(a, b, (((1,), (1,)), ((), ())), preferred_element_type=F32)


def dot_tn(a, b):
    return lax.dot_general(a, b, (((0,), (0,)), ((), ())), preferred_element_type=F32)


def ones_where(mask):
    return jnp.where(mask, 1.0, 0.0).astype(BF16)


def sigmoid(x):
    return 0.5 * jnp.tanh(0.5 * x) + 0.5


def kernel(
    mem_hbm, feat_hbm, dest_hbm, slot_hbm, nbr_hbm, wmsg_hbm, win_hbm, whid_hbm, wq_hbm, wkv_hbm, wout_hbm,
    new_ref, emb_ref,
    mem_ref, feat_ref, dest_ref, slot_ref, nbr_ref, wmsg_ref, win, whid, wqkv, order, wout,
    tail, wtail, ev_out, ev_in, gh, sums, cnt,
    mean_msg, w_both, row_hot, cell_hot, bkt, wanted, table, ind, tabs, reqs, celltab, cmat,
    stats, blocks, picks, to_left, to_right, q_ref, vals, scores, probs, widen_all,
    w_sem, ev_send, ev_recv, rq_send, rq_recv, bl_send, bl_recv, pk_send, pk_recv,
):
    group, dev = lax.axis_index("group"), lax.axis_index("dev")
    y, x = dev // SIDE, dev % SIDE
    left, right = (group + RANGES - 1) % RANGES, (group + 1) % RANGES

    def owner(dy, dx):
        return ((y + dy) % SIDE) * SIDE + (x + dx) % SIDE

    def event_owner(k):
        dy = k % 8 // 2
        return owner(dy, k % 2 * 2 + (dy + k // 8) % 2)

    def finish(part, sem):
        pltpu.make_async_copy(part, part, sem).wait()

    barrier = pltpu.get_barrier_semaphore()

    for side in (left, right):
        pl.semaphore_signal(barrier, inc=1, device_id=(side, dev), device_id_type=MESH)

    def greet(k, _):
        pl.semaphore_signal(
            barrier, inc=1, device_id=(group, event_owner(k)), device_id_type=MESH
        )
        return 0

    lax.fori_loop(1, OWNERS, greet, 0)

    loads = [
        pltpu.make_async_copy(src, dst, w_sem.at[i])
        for i, (src, dst) in enumerate(
            (
                (whid_hbm, whid),
                (win_hbm, win),
                (wq_hbm, wqkv.at[0]),
                (wkv_hbm.at[:, pl.ds(0, WIDTH)], wqkv.at[1]),
                (wkv_hbm.at[:, pl.ds(WIDTH, WIDTH)], wqkv.at[2]),
                (feat_hbm, feat_ref),
                (dest_hbm, dest_ref),
                (slot_hbm, slot_ref),
                (nbr_hbm, nbr_ref),
                (mem_hbm, mem_ref),
                (wmsg_hbm, wmsg_ref),
                (wout_hbm, wout.at[0]),
            )
        )
    ]
    for load in loads[5:] + loads[:5]:
        load.start()
    for load in loads[5:8]:
        load.wait()

    tail[...] = jnp.zeros_like(tail)
    tail[0:TAIL, :] = feat_ref[128:FEAT, :].astype(F32)
    tail[TAIL : TAIL + 1, :] = (slot_ref[...] + 1).astype(F32)
    tails = tail[...].astype(BF16)
    blank = jnp.zeros((64, EVENTS), BF16)
    head = feat_ref[0:128, :]
    feats = (
        jnp.concatenate([head, tails, blank], axis=0),
        jnp.concatenate([head, blank, tails], axis=0),
    )
    dest = dest_ref[...]
    mine = iota((OWNERS, EVENTS), 0) == dest
    upper = ones_where(iota((EVENTS, EVENTS), 0) < iota((EVENTS, EVENTS), 1))
    before = dot(ones_where(mine), upper)
    place = jnp.sum(jnp.where(mine, before, 0.0), axis=0, keepdims=True).astype(I32) + dest * CAP

    def ev_copy(k):
        return pltpu.make_async_remote_copy(
            src_ref=ev_out.at[k],
            dst_ref=ev_in.at[k],
            send_sem=ev_send.at[0],
            recv_sem=ev_recv.at[k // 8],
            device_id=(group, event_owner(k)),
            device_id_type=MESH,
        )

    def pack(i, _):
        rows = SIDE - 1 - i
        packed = []
        for part in range(2):
            pick = [
                iota((HALF, EVENTS), 0) == place - (event_owner(rows * SIDE + column) * CAP + part * HALF)
                for column in range(SIDE)
            ]
            pick = jnp.concatenate([ones_where(one) for one in pick], axis=0)
            packed.append(dot_nt(pick, feats[part]))
        for column in range(SIDE):
            k = rows * SIDE + column
            at = slice(column * HALF, (column + 1) * HALF)
            ev_out[k, 0:HALF, :] = packed[0][at, 0:128].astype(BF16)
            ev_out[k, HALF:CAP, :] = packed[1][at, 0:128].astype(BF16)
            ev_out[k, CAP:PACK, :] = (packed[0][at, 128:] + packed[1][at, 128:]).astype(BF16)
        return 0

    lax.fori_loop(0, SIDE, pack, 0)
    ev_in[0] = ev_out[0]
    pl.semaphore_wait(barrier, OWNERS - 1 + 2)

    def send_events(i, _):
        ev_copy(OWNERS - 1 - i).start()
        return 0

    lax.fori_loop(0, 8, send_events, 0)

    loads[8].wait()
    ids = nbr_ref[...]
    role = ((ids >> 12) - group + 1 + RANGES) % RANGES
    named = (ids >> 8) & 15
    rel = (((named >> 2) - y) & 3) * SIDE + ((named - x) & 3)
    slot_of = jnp.zeros_like(rel)
    for number, (dy, dx) in enumerate(ORDER):
        slot_of = jnp.where(rel == dy * SIDE + dx, number, slot_of)
    bucket = slot_of * ROLES + role
    bkt[...] = bucket
    wanted[...] = (ids & 255) + 1
    ahead = ones_where(iota((CELLS, CELLS), 0) < iota((CELLS, CELLS), 1))
    bucket_ids, place_ids = iota((BUCKETS, CELLS), 0), iota((LANES, CELLS), 0)
    cell = jnp.broadcast_to((iota((1, CELLS), 1) + 1).astype(F32), (BUCKETS, CELLS))
    filler = jnp.zeros((LANES - 2 * BUCKETS, CELLS), BF16)
    table[...] = jnp.zeros_like(table)

    def tabulate(i, offset):
        inside = [bucket_ids == bkt[pl.ds(i * BATCH + j, 1), :] for j in range(BATCH)]
        before = dot(jnp.concatenate([ones_where(one) for one in inside], axis=0), ahead)
        hots, boths = [], []
        for j in range(BATCH):
            rank = before[j * BUCKETS : (j + 1) * BUCKETS] + offset
            offset = offset + jnp.sum(jnp.where(inside[j], 1.0, 0.0), axis=1, keepdims=True)
            rank = jnp.sum(jnp.where(inside[j], rank, 0.0), axis=0, keepdims=True).astype(I32)
            hot = ones_where(place_ids == rank)
            at = pl.ds(pl.multiple_of((i * BATCH + j) * CELLS, CELLS), CELLS)
            ind[0:LANES, at] = hot
            ind[LANES : 2 * LANES, at] = hot
            row = wanted[pl.ds(i * BATCH + j, 1), :].astype(F32)
            asked = jnp.where(inside[j], row, 0.0).astype(BF16)
            by = jnp.where(inside[j], cell, 0.0).astype(BF16)
            hots.append(hot)
            boths.append(jnp.concatenate([asked, by, filler], axis=0))
        table[...] += dot_nt(jnp.concatenate(hots, axis=1), jnp.concatenate(boths, axis=1))
        return offset

    lax.fori_loop(0, NBR // BATCH, tabulate, jnp.zeros((BUCKETS, 1), F32))
    lax.fori_loop(8, OWNERS - 1, send_events, 0)
    tabs[...] = table[...].astype(BF16)
    celltab[...] = table[...].T[BUCKETS : 2 * BUCKETS, :]

    asks = [
        pltpu.make_async_remote_copy(
            src_ref=tabs,
            dst_ref=reqs.at[i],
            send_sem=rq_send.at[i],
            recv_sem=rq_recv.at[i],
            device_id=(side, dev),
            device_id_type=MESH,
        )
        for i, side in enumerate((right, left))
    ]
    for ask in asks:
        ask.start()

    every = jnp.ones((LANES, CELLS), BF16)

    def chosen(*wanted):
        lane = iota((ROWS, LANES), 1)
        columns = [
            jnp.where(lane == column, tab[0:ROWS, :].astype(F32), 0.0).astype(BF16)
            for tab, column in wanted
        ]
        rows = ROWS * len(columns)
        values = dot(jnp.concatenate(columns, axis=0), every)
        return ones_where(values == (iota((rows, CELLS), 1) + 1).astype(F32))

    def own_tables(i, _):
        for s in (2 * i, 2 * i + 1):
            first = s * ROLES
            hot = chosen(
                (tabs, BUCKETS + first),
                (tabs, BUCKETS + first + 1),
                (tabs, BUCKETS + first + 2),
                (tabs, first + 1),
            )
            cell_hot[s] = hot[0 : ROLES * ROWS]
            row_hot[s, 2 * ROWS : 3 * ROWS, :] = hot[ROLES * ROWS :]
        return 0

    lax.fori_loop(0, OWNERS // 2, own_tables, 0)
    loads[9].wait()
    loads[10].wait()
    loads[0].wait()

    def hidden(part, _):
        columns = pl.ds(pl.multiple_of(part * WIDTH, WIDTH), WIDTH)
        gh[:, columns] = dot(mem_ref[...], whid[:, columns])
        return 0

    lax.fori_loop(0, 3, hidden, 0)

    column = iota((1, WIDTH), 1)
    order[...] = ones_where(
        iota((WIDTH, WIDTH), 0) == (column % HEADS) * HEAD + column // HEADS
    )
    for load in loads[2:5]:
        load.wait()

    def reorder(part, _):
        wqkv[part] = dot(wqkv[part], order[...]).astype(BF16)
        return 0

    lax.fori_loop(0, 3, reorder, 0)

    wtail[...] = jnp.zeros_like(wtail)
    wtail[0:TAIL, :] = wmsg_ref[128:FEAT, :].astype(F32)
    w_tail = wtail[...].astype(BF16)
    w_blank = jnp.zeros((64, WIDTH), BF16)
    w_both[0] = jnp.concatenate([wmsg_ref[0:128, :], w_tail, w_blank], axis=0)
    w_both[1] = jnp.concatenate([wmsg_ref[0:128, :], w_blank, w_tail], axis=0)

    sums[...] = jnp.zeros_like(sums)
    cnt[...] = jnp.zeros_like(cnt)

    def collect(i, _):
        first = (1 - i) * 8

        @pl.when(i == 0)
        def _():
            finish(ev_in.at[pl.ds(8, 8)], ev_recv.at[1])

        @pl.when(i == 1)
        def _():
            finish(ev_in.at[pl.ds(1, 7)], ev_recv.at[0])

        tail_in = ev_in[pl.ds(first, 8), CAP:PACK, :].reshape(8 * HALF, 128)
        for part in range(2):
            main = ev_in[pl.ds(first, 8), part * HALF : (part + 1) * HALF, :]
            main = main.reshape(8 * HALF, 128)
            raw = dot(jnp.concatenate([main, tail_in], axis=1), w_both[part])
            half = 0.5 * raw
            message = (half + half * jnp.tanh(half)).astype(BF16)
            column = ones_where(iota((16, 128), 1) == 64 * part + TAIL)
            marks = dot_nt(column, tail_in)[0:1, :]
            here = (iota((CELLS, 8 * HALF), 0) + 1).astype(F32) == marks
            sums[...] += dot(ones_where(here), message)
            cnt[...] += jnp.sum(jnp.where(here, 1.0, 0.0), axis=1, keepdims=True)
        return 0

    lax.fori_loop(0, 2, collect, 0)
    mean_msg[...] = (sums[...] / jnp.maximum(cnt[:, 0:1], 1.0)).astype(BF16)
    loads[1].wait()

    def update(tile, _):
        def columns(gate):
            return pl.ds(pl.multiple_of(gate * WIDTH + tile * TILE, TILE), TILE)

        mean = mean_msg[...]
        gate_z = sigmoid(dot(mean, win[:, columns(0)]) + gh[:, columns(0)])
        gate_r = sigmoid(dot(mean, win[:, columns(1)]) + gh[:, columns(1)])
        cand = jnp.tanh(dot(mean, win[:, columns(2)]) + gate_r * gh[:, columns(2)])
        old = mem_ref[:, columns(0)].astype(F32)
        updated = (1.0 - gate_z) * old + gate_z * cand
        new_memory = jnp.where(cnt[:, 0:1] > 0, updated, old).astype(BF16)
        blocks[0, :, columns(0)] = new_memory
        new_ref[:, columns(0)] = new_memory
        return 0

    lax.fori_loop(0, WIDTH // TILE, update, 0)

    def bl_copy(number):
        source, target, first, rows, (dy, dx) = MESSAGES[number]
        return pltpu.make_async_remote_copy(
            src_ref=blocks.at[source, pl.ds(first, rows)],
            dst_ref=blocks.at[target, pl.ds(first, rows)],
            send_sem=bl_send.at[0],
            recv_sem=bl_recv.at[GROUP_OF[number]],
            device_id=(group, owner(dy, dx)),
            device_id_type=MESH,
        )

    def pk_copy(side, s):
        source, first, target = ((to_right, 0, right), (to_left, 2 * ROWS, left))[side]
        return pltpu.make_async_remote_copy(
            src_ref=source.at[s],
            dst_ref=picks.at[s, pl.ds(first, ROWS)],
            send_sem=pk_send.at[side],
            recv_sem=pk_recv.at[(s + 1) // 2],
            device_id=(target, dev),
            device_id_type=MESH,
        )

    def arrived(awaited):
        rows = sum(MESSAGES[number][3] for number in awaited)
        if rows > CELLS:
            part = blocks.at[pl.ds(0, rows // CELLS)]
        else:
            part = blocks.at[0, pl.ds(0, rows)]
        finish(part, bl_recv.at[GROUP_OF[awaited[0]]])

    for number in START:
        bl_copy(number).start()
    q_ref[...] = (dot(blocks[0], wqkv[0]) * (HEAD**-0.5)).astype(BF16)

    loads[11].wait()
    wout[1] = dot_tn(order[...], wout[0]).astype(BF16)
    for ask in asks:
        ask.wait_recv()

    def requested(i, _):
        for s in (2 * i, 2 * i + 1):
            row_hot[s, 0 : 2 * ROWS, :] = chosen(
                (reqs.at[1], s * ROLES), (reqs.at[0], s * ROLES + 2)
            )
            for r in range(ROLES):
                row = celltab[pl.ds(s * ROLES + r, 1), :]
                hot = ones_where((iota((CELLS, LANES), 0) + 1).astype(F32) == row)
                cmat[s, :, r * LANES : (r + 1) * LANES] = hot
                vals[s, r * LANES + ROWS : (r + 1) * LANES, :] = blank_rows
        return 0

    blank_rows = jnp.zeros((LANES - ROWS, WIDTH), BF16)
    lax.fori_loop(0, OWNERS // 2, requested, 0)

    head_rows = ones_where(iota((16, 2 * LANES), 1) % HEADS == iota((16, 2 * LANES), 0))

    widen = ones_where(iota((HEADS, WIDTH), 0) == iota((HEADS, WIDTH), 1) % HEADS)
    group_heads = 2 * ROLES * HEADS
    lane = iota((group_heads, 2 * ROLES * LANES), 1)
    head_of = lane // LANES * HEADS + lane % HEADS
    widen_all[...] = ones_where(iota((group_heads, 2 * ROLES * LANES), 0) == head_of)

    def entries(j):
        return pl.ds(pl.multiple_of(j * CELLS, CELLS), CELLS)

    def attend(begin, end):
        low, high = begin * ROLES, end * ROLES
        rows = slice(low * HEADS, high * HEADS)
        part = scores[rows, :]
        upper_part = part.astype(BF16)
        lower_part = (part - upper_part.astype(F32)).astype(BF16)
        parts = jnp.concatenate([upper_part, lower_part], axis=1)
        numbers = lax.broadcasted_iota(I32, (high - low, HEADS, CELLS), 0) + low

        def order_by_cell(i, top):
            for j in range(BATCH):
                j = i * BATCH + j
                found = dot(parts, ind[:, entries(j)]).reshape(high - low, HEADS, CELLS)
                bucket = bkt[pl.ds(j, 1), :]
                inside = numbers == bucket.reshape(1, 1, CELLS)
                mine = jnp.sum(jnp.where(inside, found, 0.0), axis=0)
                mine = jnp.where(jnp.logical_and(bucket >= low, bucket < high), mine, LOWEST)
                probs[j] = mine
                top = jnp.maximum(top, mine)
            return top

        lowest = jnp.full((HEADS, CELLS), LOWEST, F32)
        top = lax.fori_loop(0, NBR // BATCH, order_by_cell, lowest)
        if begin > 0:
            top = jnp.maximum(top, stats[0])
        found = probs[...]
        raised = jnp.where(found == LOWEST, 0.0, jnp.exp(found - top[None]))
        total = jnp.sum(raised, axis=0)
        if begin > 0:
            scale = jnp.exp(stats[0] - top)
            total = total + stats[1] * scale
            if end == OWNERS:
                inverse = 1.0 / total
                raised = raised * inverse[None]
                scale = scale * inverse
            upper_part = scale.astype(BF16)
            lower_part = (scale - upper_part.astype(F32)).astype(BF16)
            sums[...] = sums[...] * (dot_tn(upper_part, widen) + dot_tn(lower_part, widen))
        else:
            sums[...] = jnp.zeros_like(sums)
        stats[0] = top
        stats[1] = total
        probs[...] = raised
        scores[rows, :] = jnp.zeros_like(part)

        def order_by_bucket(i, _):
            placed = []
            for j in range(BATCH):
                j = i * BATCH + j
                inside = numbers == bkt[pl.ds(j, 1), :].reshape(1, 1, CELLS)
                one = jnp.where(inside, probs[j][None], 0.0)
                placed.append(one.reshape((high - low) * HEADS, CELLS).astype(BF16))
            part = pl.ds(pl.multiple_of(i * BATCH * CELLS, BATCH * CELLS), BATCH * CELLS)
            scores[rows, :] += dot_nt(jnp.concatenate(placed, axis=1), ind[0:LANES, part])
            return 0

        lax.fori_loop(0, NBR // BATCH, order_by_bucket, 0)

        def weigh(i, _):
            weighted = []
            first = pl.multiple_of(i * group_heads, group_heads)
            weights = scores[pl.ds(first, group_heads), :].T.astype(BF16)
            wide = dot(weights, widen_all[...]).astype(BF16)
            for r in range(2 * ROLES):
                value = vals[2 * i + r // ROLES, (r % ROLES) * LANES : (r % ROLES + 1) * LANES, :]
                weight = wide[:, r * LANES : (r + 1) * LANES]
                weight = jnp.concatenate([weight] * (WIDTH // LANES), axis=1)
                weighted.append(weight * value)
            cells = jnp.concatenate([cmat[2 * i], cmat[2 * i + 1]], axis=1)
            sums[...] += dot(cells, jnp.concatenate(weighted, axis=0))
            return 0

        lax.fori_loop(begin // 2, end // 2, weigh, 0)

    def pick_rows(s):
        got = dot(row_hot[s], blocks[s]).astype(BF16)
        to_right[s] = got[0:ROWS]
        pk_copy(0, s).start()
        to_left[s] = got[ROWS : 2 * ROWS]
        pk_copy(1, s).start()
        picks[s, ROWS : 2 * ROWS, :] = got[2 * ROWS : 3 * ROWS]

    def score_slots(t, number):
        finish(to_left.at[pl.ds(0, 2 * number)], pk_recv.at[(t + 1) // 2])
        picked = picks[pl.ds(t, number)].reshape(number * ROLES * ROWS, WIDTH)
        owned = cell_hot[pl.ds(t, number)].reshape(number * ROLES * ROWS, CELLS)
        keys = dot(picked, wqkv[1]).astype(BF16).astype(F32)
        product = dot(owned, q_ref[...]) * keys
        tiles = [product[:, i * LANES : (i + 1) * LANES] for i in range(WIDTH // LANES)]
        product = (tiles[0] + tiles[1]) + (tiles[2] + tiles[3])
        upper_part = product.astype(BF16)
        lower_part = (product - upper_part.astype(F32)).astype(BF16)
        split = jnp.concatenate([upper_part, lower_part], axis=1)
        values = dot(picked, wqkv[2]).astype(BF16)
        for r in range(number * ROLES):
            rows = slice(r * ROWS, (r + 1) * ROWS)
            first = pl.multiple_of((t * ROLES + r) * HEADS, HEADS)
            scores[pl.ds(first, HEADS), 0:ROWS] = dot_nt(head_rows, split[rows])[0:HEADS]
            vals[t + r // ROLES, (r % ROLES) * LANES : (r % ROLES) * LANES + ROWS, :] = values[rows]

    def step(s, _):
        @pl.when(s < OWNERS)
        def _():
            for at, stages in STEPS.items():

                @pl.when(s == at)
                def _(stages=stages):
                    for awaited, sent in stages:
                        arrived(awaited)
                        for number in sent:
                            bl_copy(number).start()

            pick_rows(s)

        for after, begin, end in EARLY:

            @pl.when(s == after)
            def _(begin=begin, end=end):
                attend(begin, end)

        @pl.when(jnp.logical_and(jnp.logical_and(s >= LAG, s < OWNERS + LAG - 2), s % 2 == 1))
        def _():
            score_slots(s - LAG + 1, 2)

        @pl.when(jnp.logical_or(s == LAG - 1, s == OWNERS + LAG - 2))
        def _():
            score_slots((s // OWNERS) * (OWNERS - 1), 1)

        return 0

    lax.fori_loop(0, OWNERS + LAG - 1, step, 0)

    attend(*LAST)
    attended = sums[...].astype(BF16)
    emb_ref[...] = (blocks[0].astype(F32) + dot(attended, wout[1])).astype(BF16)

    finish(ev_out.at[pl.ds(1, OWNERS - 1)], ev_send.at[0])
    for ask in asks:
        ask.wait_send()
    finish(blocks.at[pl.ds(0, SENT_BLOCKS)], bl_send.at[0])
    finish(to_right, pk_send.at[0])
    finish(to_left, pk_send.at[1])


def hand_over(new_in, emb_in, new_ref, emb_ref):
    new_ref[...] = new_in[...]
    emb_ref[...] = emb_in[...]


def body(memory, features, dest, slot, neighbours, w_message, w_input, w_hidden, w_query, w_keyval, w_output):
    inside = pl.BlockSpec(memory_space=pltpu.VMEM)
    outside = pl.BlockSpec(memory_space=pl.ANY)
    vmem, dma = pltpu.VMEM, pltpu.SemaphoreType.DMA
    results = pl.pallas_call(
        kernel,
        out_shape=(
            jax.ShapeDtypeStruct((CELLS, WIDTH), BF16),
            jax.ShapeDtypeStruct((CELLS, WIDTH), BF16),
        ),
        in_specs=[outside] * 11,
        out_specs=(inside, inside),
        scratch_shapes=[
            vmem((CELLS, WIDTH), BF16),
            vmem((FEAT, EVENTS), BF16),
            vmem((1, EVENTS), I32),
            vmem((1, EVENTS), I32),
            vmem((NBR, CELLS), I32),
            vmem((FEAT, WIDTH), BF16),
            vmem((WIDTH, 3 * WIDTH), BF16),
            vmem((WIDTH, 3 * WIDTH), BF16),
            vmem((3, WIDTH, WIDTH), BF16),
            vmem((WIDTH, WIDTH), BF16),
            vmem((2, WIDTH, WIDTH), BF16),
            vmem((64, EVENTS), F32),
            vmem((64, WIDTH), F32),
            vmem((OWNERS, PACK, 128), BF16),
            vmem((OWNERS, PACK, 128), BF16),
            vmem((CELLS, 3 * WIDTH), F32),
            vmem((CELLS, WIDTH), F32),
            vmem((CELLS, LANES), F32),
            vmem((CELLS, WIDTH), BF16),
            vmem((2, 256, WIDTH), BF16),
            vmem((OWNERS, ROLES * ROWS, CELLS), BF16),
            vmem((OWNERS, ROLES * ROWS, CELLS), BF16),
            vmem((NBR, CELLS), I32),
            vmem((NBR, CELLS), I32),
            vmem((LANES, LANES), F32),
            vmem((2 * LANES, NBR * CELLS), BF16),
            vmem((LANES, LANES), BF16),
            vmem((2, LANES, LANES), BF16),
            vmem((BUCKETS, LANES), F32),
            vmem((OWNERS, CELLS, ROLES * LANES), BF16),
            vmem((2, HEADS, CELLS), F32),
            vmem((OWNERS, CELLS, WIDTH), BF16),
            vmem((OWNERS, ROLES * ROWS, WIDTH), BF16),
            vmem((OWNERS, ROWS, WIDTH), BF16),
            vmem((OWNERS, ROWS, WIDTH), BF16),
            vmem((CELLS, WIDTH), BF16),
            vmem((OWNERS, ROLES * LANES, WIDTH), BF16),
            vmem((BUCKETS * HEADS, LANES), F32),
            vmem((NBR, HEADS, CELLS), F32),
            vmem((2 * ROLES * HEADS, 2 * ROLES * LANES), BF16),
            dma((12,)),
            dma((1,)),
            dma((2,)),
            dma((2,)),
            dma((2,)),
            dma((1,)),
            dma((len(GROUPS),)),
            dma((2,)),
            dma((OWNERS // 2 + 1,)),
        ],
        compiler_params=pltpu.CompilerParams(
            collective_id=0, has_side_effects=True, vmem_limit_bytes=58 * 1024 * 1024
        ),
        cost_estimate=pl.CostEstimate(
            flops=12_000_000_000, bytes_accessed=6_000_000, transcendentals=2_000_000
        ),
    )(
        memory,
        features.T,
        dest.reshape(1, EVENTS),
        slot.reshape(1, EVENTS),
        neighbours.T,
        w_message,
        w_input,
        w_hidden,
        w_query,
        w_keyval,
        w_output,
    )
    return pl.pallas_call(
        hand_over,
        out_shape=(
            jax.ShapeDtypeStruct((CELLS, WIDTH), BF16),
            jax.ShapeDtypeStruct((CELLS, WIDTH), BF16),
        ),
        in_specs=[inside] * 2,
        out_specs=(inside, inside),
    )(*results)


def solution(mesh):
    rows = P(("group", "dev"), None)
    placed = (rows, rows, rows, P(("group", "dev")), rows) + (P(),) * 6
    return jax.shard_map(
        body, mesh=mesh, in_specs=placed, out_specs=(rows, rows), check_vma=False
    )
```

```python
import jax
import jax.numpy as jnp
from jax import lax
from jax.experimental import pallas as pl
from jax.experimental.pallas import tpu as pltpu
from jax.sharding import PartitionSpec as P

MESH = pl.DeviceIdType.MESH
F32, BF16, I32 = jnp.float32, jnp.bfloat16, jnp.int32

HEADS = 8
HEAD = 64
NBR = 20
CELLS = 256
WIDTH = 512
EVENTS = 512
CAP = 96
HALF = CAP // 2
PACK = CAP + HALF
FEAT = 172
TAIL = FEAT - 128
ROWS = 112
LANES = 128
ROLES = 3
OWNERS = 16
SIDE = 4
RANGES = 16
BUCKETS = OWNERS * ROLES
TILE = 256
LAG = 7
EARLY = ((16, 0, 10),)
LAST = (10, 16)
LOWEST = -3.0e38
BATCH = 4

ORDER = (
    (0, 0), (0, 3), (0, 1), (3, 0), (1, 0), (3, 3), (1, 1), (0, 2),
    (2, 0), (3, 1), (1, 3), (3, 2), (1, 2), (2, 3), (2, 1), (2, 2),
)
SLOT = {rel: slot for slot, rel in enumerate(ORDER)}


def gather_plan():
    names, messages = {}, []

    def add(name, source, hop, first, rows):
        target = ((source[0] - hop[0]) % SIDE, (source[1] - hop[1]) % SIDE)
        names[name] = len(messages)
        messages.append((SLOT[source], SLOT[target], first, rows, hop))

    for cls in "ab":
        base = 0 if cls == "a" else 128

        def at(first, second, cls=cls):
            return (second % SIDE, first % SIDE) if cls == "a" else (first % SIDE, second % SIDE)

        for sign in (1, -1):
            add((cls, 1, 0, sign), at(0, 0), at(sign, 0), base, 128)
            add((cls, 2, 0, sign), at(-sign, 0), at(sign, 0), base + (0 if sign > 0 else 64), 64)
            for off in (0, -1, 1, 2):
                add((cls, 3, off, sign), at(off, 0), at(0, sign), base, 128)
                first = base + (0 if sign > 0 else 64)
                add((cls, 4, off, sign), at(off, -sign), at(0, sign), first, 64)

    def both(*items):
        return [names[(cls,) + item] for item in items for cls in "ab"]

    start = both((1, 0, 1), (1, 0, -1), (3, 0, 1), (3, 0, -1))
    steps = {
        1: [
            (
                both((1, 0, 1), (1, 0, -1)),
                both((2, 0, 1), (2, 0, -1), (3, -1, 1), (3, 1, -1)),
            ),
            (
                both((3, 0, 1), (3, 0, -1)),
                both((4, 0, 1), (4, 0, -1), (3, 1, 1), (3, -1, -1)),
            ),
        ],
        3: [(both((2, 0, 1), (2, 0, -1)), both((3, 2, 1), (3, 2, -1)))],
        5: [(both((3, -1, 1)), both((4, -1, 1)))],
        6: [(both((3, 1, -1)), both((4, 1, -1)))],
        7: [([names[("b", 4, 0, 1)], names[("b", 4, 0, -1)]], [])],
        8: [([names[("a", 4, 0, 1)], names[("a", 4, 0, -1)]], [])],
        9: [
            (
                [names[("a", 3, 1, 1)], names[("b", 3, -1, -1)]],
                [names[("a", 4, 1, 1)], names[("b", 4, -1, -1)]],
            )
        ],
        10: [
            (
                [names[("a", 3, -1, -1)], names[("b", 3, 1, 1)]],
                [names[("a", 4, -1, -1)], names[("b", 4, 1, 1)]],
            )
        ],
        11: [
            (both((3, 2, 1), (3, 2, -1)), both((4, 2, 1), (4, 2, -1))),
            ([names[("b", 4, -1, 1)], names[("b", 4, -1, -1)]], []),
        ],
        12: [([names[("b", 4, 1, 1)], names[("b", 4, 1, -1)]], [])],
        13: [([names[("a", 4, -1, 1)], names[("a", 4, -1, -1)]], [])],
        14: [([names[("a", 4, 1, 1)], names[("a", 4, 1, -1)]], [])],
        15: [(both((4, 2, 1), (4, 2, -1)), [])],
    }
    return messages, start, steps


MESSAGES, START, STEPS = gather_plan()
COUNT = len(MESSAGES)
GROUPS = [awaited for stages in STEPS.values() for awaited, _ in stages]
GROUP_OF = {number: group for group, awaited in enumerate(GROUPS) for number in awaited}
SENT_BLOCKS = sum(message[3] for message in MESSAGES) // CELLS


def iota(shape, dim):
    return lax.broadcasted_iota(I32, shape, dim)


def dot(a, b):
    return jnp.dot(a, b, preferred_element_type=F32)


def dot_nt(a, b):
    return lax.dot_general(a, b, (((1,), (1,)), ((), ())), preferred_element_type=F32)


def dot_tn(a, b):
    return lax.dot_general(a, b, (((0,), (0,)), ((), ())), preferred_element_type=F32)


def ones_where(mask):
    return jnp.where(mask, 1.0, 0.0).astype(BF16)


def sigmoid(x):
    return 0.5 * jnp.tanh(0.5 * x) + 0.5


def kernel(
    mem_hbm, feat_ref, dest_hbm, slot_hbm, nbr_hbm, wmsg_ref, win_hbm, whid_hbm, wq_hbm, wkv_hbm, wout_hbm,
    new_ref, emb_ref,
    mem_ref, dest_ref, slot_ref, nbr_ref, win, whid, wqkv, order, wout,
    tail, wtail, ev_out, ev_in, gh, sums, cnt,
    mean_msg, w_both, row_hot, cell_hot, bkt, wanted, table, ind, tabs, reqs, celltab, cmat,
    stats, blocks, picks, to_left, to_right, q_ref, vals, scores, probs, widen_all,
    w_sem, ev_send, ev_recv, rq_send, rq_recv, bl_send, bl_recv, pk_send, pk_recv,
):
    group, dev = lax.axis_index("group"), lax.axis_index("dev")
    y, x = dev // SIDE, dev % SIDE
    left, right = (group + RANGES - 1) % RANGES, (group + 1) % RANGES

    def owner(dy, dx):
        return ((y + dy) % SIDE) * SIDE + (x + dx) % SIDE

    def event_owner(k):
        dy = k % 8 // 2
        return owner(dy, k % 2 * 2 + (dy + k // 8) % 2)

    def finish(part, sem):
        pltpu.make_async_copy(part, part, sem).wait()

    barrier = pltpu.get_barrier_semaphore()

    for side in (left, right):
        pl.semaphore_signal(barrier, inc=1, device_id=(side, dev), device_id_type=MESH)

    def greet(k, _):
        pl.semaphore_signal(
            barrier, inc=1, device_id=(group, event_owner(k)), device_id_type=MESH
        )
        return 0

    lax.fori_loop(1, OWNERS, greet, 0)

    loads = [
        pltpu.make_async_copy(src, dst, w_sem.at[i])
        for i, (src, dst) in enumerate(
            (
                (whid_hbm, whid),
                (win_hbm, win),
                (wq_hbm, wqkv.at[0]),
                (wkv_hbm.at[:, pl.ds(0, WIDTH)], wqkv.at[1]),
                (wkv_hbm.at[:, pl.ds(WIDTH, WIDTH)], wqkv.at[2]),
                (dest_hbm, dest_ref),
                (slot_hbm, slot_ref),
                (nbr_hbm, nbr_ref),
                (mem_hbm, mem_ref),
                (wout_hbm, wout.at[0]),
            )
        )
    ]
    for load in loads[5:] + loads[:5]:
        load.start()
    for load in loads[5:7]:
        load.wait()

    tail[...] = jnp.zeros_like(tail)
    tail[0:TAIL, :] = feat_ref[128:FEAT, :].astype(F32)
    tail[TAIL : TAIL + 1, :] = (slot_ref[...] + 1).astype(F32)
    tails = tail[...].astype(BF16)
    blank = jnp.zeros((64, EVENTS), BF16)
    head = feat_ref[0:128, :]
    feats = (
        jnp.concatenate([head, tails, blank], axis=0),
        jnp.concatenate([head, blank, tails], axis=0),
    )
    dest = dest_ref[...]
    mine = iota((OWNERS, EVENTS), 0) == dest
    upper = ones_where(iota((EVENTS, EVENTS), 0) < iota((EVENTS, EVENTS), 1))
    before = dot(ones_where(mine), upper)
    place = jnp.sum(jnp.where(mine, before, 0.0), axis=0, keepdims=True).astype(I32) + dest * CAP

    def ev_copy(k):
        return pltpu.make_async_remote_copy(
            src_ref=ev_out.at[k],
            dst_ref=ev_in.at[k],
            send_sem=ev_send.at[0],
            recv_sem=ev_recv.at[k // 8],
            device_id=(group, event_owner(k)),
            device_id_type=MESH,
        )

    def pack(i, _):
        rows = SIDE - 1 - i
        packed = []
        for part in range(2):
            pick = [
                iota((HALF, EVENTS), 0) == place - (event_owner(rows * SIDE + column) * CAP + part * HALF)
                for column in range(SIDE)
            ]
            pick = jnp.concatenate([ones_where(one) for one in pick], axis=0)
            packed.append(dot_nt(pick, feats[part]))
        for column in range(SIDE):
            k = rows * SIDE + column
            at = slice(column * HALF, (column + 1) * HALF)
            ev_out[k, 0:HALF, :] = packed[0][at, 0:128].astype(BF16)
            ev_out[k, HALF:CAP, :] = packed[1][at, 0:128].astype(BF16)
            ev_out[k, CAP:PACK, :] = (packed[0][at, 128:] + packed[1][at, 128:]).astype(BF16)
        return 0

    lax.fori_loop(0, SIDE, pack, 0)
    ev_in[0] = ev_out[0]
    pl.semaphore_wait(barrier, OWNERS - 1 + 2)

    def send_events(i, _):
        ev_copy(OWNERS - 1 - i).start()
        return 0

    lax.fori_loop(0, 8, send_events, 0)

    loads[7].wait()
    ids = nbr_ref[...]
    role = ((ids >> 12) - group + 1 + RANGES) % RANGES
    named = (ids >> 8) & 15
    rel = (((named >> 2) - y) & 3) * SIDE + ((named - x) & 3)
    slot_of = jnp.zeros_like(rel)
    for number, (dy, dx) in enumerate(ORDER):
        slot_of = jnp.where(rel == dy * SIDE + dx, number, slot_of)
    bucket = slot_of * ROLES + role
    bkt[...] = bucket
    wanted[...] = (ids & 255) + 1
    ahead = ones_where(iota((CELLS, CELLS), 0) < iota((CELLS, CELLS), 1))
    bucket_ids, place_ids = iota((BUCKETS, CELLS), 0), iota((LANES, CELLS), 0)
    cell = jnp.broadcast_to((iota((1, CELLS), 1) + 1).astype(F32), (BUCKETS, CELLS))
    filler = jnp.zeros((LANES - 2 * BUCKETS, CELLS), BF16)
    table[...] = jnp.zeros_like(table)

    def tabulate(i, offset):
        inside = [bucket_ids == bkt[pl.ds(i * BATCH + j, 1), :] for j in range(BATCH)]
        before = dot(jnp.concatenate([ones_where(one) for one in inside], axis=0), ahead)
        hots, boths = [], []
        for j in range(BATCH):
            rank = before[j * BUCKETS : (j + 1) * BUCKETS] + offset
            offset = offset + jnp.sum(jnp.where(inside[j], 1.0, 0.0), axis=1, keepdims=True)
            rank = jnp.sum(jnp.where(inside[j], rank, 0.0), axis=0, keepdims=True).astype(I32)
            hot = ones_where(place_ids == rank)
            at = pl.ds(pl.multiple_of((i * BATCH + j) * CELLS, CELLS), CELLS)
            ind[0:LANES, at] = hot
            ind[LANES : 2 * LANES, at] = hot
            row = wanted[pl.ds(i * BATCH + j, 1), :].astype(F32)
            asked = jnp.where(inside[j], row, 0.0).astype(BF16)
            by = jnp.where(inside[j], cell, 0.0).astype(BF16)
            hots.append(hot)
            boths.append(jnp.concatenate([asked, by, filler], axis=0))
        table[...] += dot_nt(jnp.concatenate(hots, axis=1), jnp.concatenate(boths, axis=1))
        return offset

    lax.fori_loop(0, NBR // BATCH, tabulate, jnp.zeros((BUCKETS, 1), F32))
    lax.fori_loop(8, OWNERS - 1, send_events, 0)
    tabs[...] = table[...].astype(BF16)
    celltab[...] = table[...].T[BUCKETS : 2 * BUCKETS, :]

    asks = [
        pltpu.make_async_remote_copy(
            src_ref=tabs,
            dst_ref=reqs.at[i],
            send_sem=rq_send.at[i],
            recv_sem=rq_recv.at[i],
            device_id=(side, dev),
            device_id_type=MESH,
        )
        for i, side in enumerate((right, left))
    ]
    for ask in asks:
        ask.start()

    every = jnp.ones((LANES, CELLS), BF16)

    def chosen(*wanted):
        lane = iota((ROWS, LANES), 1)
        columns = [
            jnp.where(lane == column, tab[0:ROWS, :].astype(F32), 0.0).astype(BF16)
            for tab, column in wanted
        ]
        rows = ROWS * len(columns)
        values = dot(jnp.concatenate(columns, axis=0), every)
        return ones_where(values == (iota((rows, CELLS), 1) + 1).astype(F32))

    def own_tables(i, _):
        for s in (2 * i, 2 * i + 1):
            first = s * ROLES
            hot = chosen(
                (tabs, BUCKETS + first),
                (tabs, BUCKETS + first + 1),
                (tabs, BUCKETS + first + 2),
                (tabs, first + 1),
            )
            cell_hot[s] = hot[0 : ROLES * ROWS]
            row_hot[s, 2 * ROWS : 3 * ROWS, :] = hot[ROLES * ROWS :]
        return 0

    lax.fori_loop(0, OWNERS // 2, own_tables, 0)
    loads[8].wait()
    loads[0].wait()

    def hidden(part, _):
        columns = pl.ds(pl.multiple_of(part * WIDTH, WIDTH), WIDTH)
        gh[:, columns] = dot(mem_ref[...], whid[:, columns])
        return 0

    lax.fori_loop(0, 3, hidden, 0)

    column = iota((1, WIDTH), 1)
    order[...] = ones_where(
        iota((WIDTH, WIDTH), 0) == (column % HEADS) * HEAD + column // HEADS
    )
    for load in loads[2:5]:
        load.wait()

    def reorder(part, _):
        wqkv[part] = dot(wqkv[part], order[...]).astype(BF16)
        return 0

    lax.fori_loop(0, 3, reorder, 0)

    wtail[...] = jnp.zeros_like(wtail)
    wtail[0:TAIL, :] = wmsg_ref[128:FEAT, :].astype(F32)
    w_tail = wtail[...].astype(BF16)
    w_blank = jnp.zeros((64, WIDTH), BF16)
    w_both[0] = jnp.concatenate([wmsg_ref[0:128, :], w_tail, w_blank], axis=0)
    w_both[1] = jnp.concatenate([wmsg_ref[0:128, :], w_blank, w_tail], axis=0)

    sums[...] = jnp.zeros_like(sums)
    cnt[...] = jnp.zeros_like(cnt)

    def collect(i, _):
        first = (1 - i) * 8

        @pl.when(i == 0)
        def _():
            finish(ev_in.at[pl.ds(8, 8)], ev_recv.at[1])

        @pl.when(i == 1)
        def _():
            finish(ev_in.at[pl.ds(1, 7)], ev_recv.at[0])

        tail_in = ev_in[pl.ds(first, 8), CAP:PACK, :].reshape(8 * HALF, 128)
        for part in range(2):
            main = ev_in[pl.ds(first, 8), part * HALF : (part + 1) * HALF, :]
            main = main.reshape(8 * HALF, 128)
            raw = dot(jnp.concatenate([main, tail_in], axis=1), w_both[part])
            half = 0.5 * raw
            message = (half + half * jnp.tanh(half)).astype(BF16)
            column = ones_where(iota((16, 128), 1) == 64 * part + TAIL)
            marks = dot_nt(column, tail_in)[0:1, :]
            here = (iota((CELLS, 8 * HALF), 0) + 1).astype(F32) == marks
            sums[...] += dot(ones_where(here), message)
            cnt[...] += jnp.sum(jnp.where(here, 1.0, 0.0), axis=1, keepdims=True)
        return 0

    lax.fori_loop(0, 2, collect, 0)
    mean_msg[...] = (sums[...] / jnp.maximum(cnt[:, 0:1], 1.0)).astype(BF16)
    loads[1].wait()

    def update(tile, _):
        def columns(gate):
            return pl.ds(pl.multiple_of(gate * WIDTH + tile * TILE, TILE), TILE)

        mean = mean_msg[...]
        gate_z = sigmoid(dot(mean, win[:, columns(0)]) + gh[:, columns(0)])
        gate_r = sigmoid(dot(mean, win[:, columns(1)]) + gh[:, columns(1)])
        cand = jnp.tanh(dot(mean, win[:, columns(2)]) + gate_r * gh[:, columns(2)])
        old = mem_ref[:, columns(0)].astype(F32)
        updated = (1.0 - gate_z) * old + gate_z * cand
        new_memory = jnp.where(cnt[:, 0:1] > 0, updated, old).astype(BF16)
        blocks[0, :, columns(0)] = new_memory
        new_ref[:, columns(0)] = new_memory
        return 0

    lax.fori_loop(0, WIDTH // TILE, update, 0)

    def bl_copy(number):
        source, target, first, rows, (dy, dx) = MESSAGES[number]
        return pltpu.make_async_remote_copy(
            src_ref=blocks.at[source, pl.ds(first, rows)],
            dst_ref=blocks.at[target, pl.ds(first, rows)],
            send_sem=bl_send.at[0],
            recv_sem=bl_recv.at[GROUP_OF[number]],
            device_id=(group, owner(dy, dx)),
            device_id_type=MESH,
        )

    def pk_copy(side, s):
        source, first, target = ((to_right, 0, right), (to_left, 2 * ROWS, left))[side]
        return pltpu.make_async_remote_copy(
            src_ref=source.at[s],
            dst_ref=picks.at[s, pl.ds(first, ROWS)],
            send_sem=pk_send.at[side],
            recv_sem=pk_recv.at[(s + 1) // 2],
            device_id=(target, dev),
            device_id_type=MESH,
        )

    def arrived(awaited):
        rows = sum(MESSAGES[number][3] for number in awaited)
        if rows > CELLS:
            part = blocks.at[pl.ds(0, rows // CELLS)]
        else:
            part = blocks.at[0, pl.ds(0, rows)]
        finish(part, bl_recv.at[GROUP_OF[awaited[0]]])

    for number in START:
        bl_copy(number).start()
    q_ref[...] = (dot(blocks[0], wqkv[0]) * (HEAD**-0.5)).astype(BF16)

    loads[9].wait()
    wout[1] = dot_tn(order[...], wout[0]).astype(BF16)
    for ask in asks:
        ask.wait_recv()

    def requested(i, _):
        for s in (2 * i, 2 * i + 1):
            row_hot[s, 0 : 2 * ROWS, :] = chosen(
                (reqs.at[1], s * ROLES), (reqs.at[0], s * ROLES + 2)
            )
            for r in range(ROLES):
                row = celltab[pl.ds(s * ROLES + r, 1), :]
                hot = ones_where((iota((CELLS, LANES), 0) + 1).astype(F32) == row)
                cmat[s, :, r * LANES : (r + 1) * LANES] = hot
                vals[s, r * LANES + ROWS : (r + 1) * LANES, :] = blank_rows
        return 0

    blank_rows = jnp.zeros((LANES - ROWS, WIDTH), BF16)
    lax.fori_loop(0, OWNERS // 2, requested, 0)

    head_rows = ones_where(iota((16, 2 * LANES), 1) % HEADS == iota((16, 2 * LANES), 0))

    widen = ones_where(iota((HEADS, WIDTH), 0) == iota((HEADS, WIDTH), 1) % HEADS)
    group_heads = 2 * ROLES * HEADS
    lane = iota((group_heads, 2 * ROLES * LANES), 1)
    head_of = lane // LANES * HEADS + lane % HEADS
    widen_all[...] = ones_where(iota((group_heads, 2 * ROLES * LANES), 0) == head_of)

    def entries(j):
        return pl.ds(pl.multiple_of(j * CELLS, CELLS), CELLS)

    def attend(begin, end):
        low, high = begin * ROLES, end * ROLES
        rows = slice(low * HEADS, high * HEADS)
        part = scores[rows, :]
        upper_part = part.astype(BF16)
        lower_part = (part - upper_part.astype(F32)).astype(BF16)
        parts = jnp.concatenate([upper_part, lower_part], axis=1)
        numbers = lax.broadcasted_iota(I32, (high - low, HEADS, CELLS), 0) + low

        def order_by_cell(i, top):
            for j in range(BATCH):
                j = i * BATCH + j
                found = dot(parts, ind[:, entries(j)]).reshape(high - low, HEADS, CELLS)
                bucket = bkt[pl.ds(j, 1), :]
                inside = numbers == bucket.reshape(1, 1, CELLS)
                mine = jnp.sum(jnp.where(inside, found, 0.0), axis=0)
                mine = jnp.where(jnp.logical_and(bucket >= low, bucket < high), mine, LOWEST)
                probs[j] = mine
                top = jnp.maximum(top, mine)
            return top

        lowest = jnp.full((HEADS, CELLS), LOWEST, F32)
        top = lax.fori_loop(0, NBR // BATCH, order_by_cell, lowest)
        if begin > 0:
            top = jnp.maximum(top, stats[0])
        found = probs[...]
        raised = jnp.where(found == LOWEST, 0.0, jnp.exp(found - top[None]))
        total = jnp.sum(raised, axis=0)
        if begin > 0:
            scale = jnp.exp(stats[0] - top)
            total = total + stats[1] * scale
            if end == OWNERS:
                inverse = 1.0 / total
                raised = raised * inverse[None]
                scale = scale * inverse
            upper_part = scale.astype(BF16)
            lower_part = (scale - upper_part.astype(F32)).astype(BF16)
            sums[...] = sums[...] * (dot_tn(upper_part, widen) + dot_tn(lower_part, widen))
        else:
            sums[...] = jnp.zeros_like(sums)
        stats[0] = top
        stats[1] = total
        probs[...] = raised
        scores[rows, :] = jnp.zeros_like(part)

        def order_by_bucket(i, _):
            placed = []
            for j in range(BATCH):
                j = i * BATCH + j
                inside = numbers == bkt[pl.ds(j, 1), :].reshape(1, 1, CELLS)
                one = jnp.where(inside, probs[j][None], 0.0)
                placed.append(one.reshape((high - low) * HEADS, CELLS).astype(BF16))
            part = pl.ds(pl.multiple_of(i * BATCH * CELLS, BATCH * CELLS), BATCH * CELLS)
            scores[rows, :] += dot_nt(jnp.concatenate(placed, axis=1), ind[0:LANES, part])
            return 0

        lax.fori_loop(0, NBR // BATCH, order_by_bucket, 0)

        def weigh(i, _):
            weighted = []
            first = pl.multiple_of(i * group_heads, group_heads)
            weights = scores[pl.ds(first, group_heads), :].T.astype(BF16)
            wide = dot(weights, widen_all[...]).astype(BF16)
            for r in range(2 * ROLES):
                value = vals[2 * i + r // ROLES, (r % ROLES) * LANES : (r % ROLES + 1) * LANES, :]
                weight = wide[:, r * LANES : (r + 1) * LANES]
                weight = jnp.concatenate([weight] * (WIDTH // LANES), axis=1)
                weighted.append(weight * value)
            cells = jnp.concatenate([cmat[2 * i], cmat[2 * i + 1]], axis=1)
            sums[...] += dot(cells, jnp.concatenate(weighted, axis=0))
            return 0

        lax.fori_loop(begin // 2, end // 2, weigh, 0)

    def pick_rows(s):
        got = dot(row_hot[s], blocks[s]).astype(BF16)
        to_right[s] = got[0:ROWS]
        pk_copy(0, s).start()
        to_left[s] = got[ROWS : 2 * ROWS]
        pk_copy(1, s).start()
        picks[s, ROWS : 2 * ROWS, :] = got[2 * ROWS : 3 * ROWS]

    def score_slots(t, number):
        finish(to_left.at[pl.ds(0, 2 * number)], pk_recv.at[(t + 1) // 2])
        picked = picks[pl.ds(t, number)].reshape(number * ROLES * ROWS, WIDTH)
        owned = cell_hot[pl.ds(t, number)].reshape(number * ROLES * ROWS, CELLS)
        keys = dot(picked, wqkv[1]).astype(BF16).astype(F32)
        product = dot(owned, q_ref[...]) * keys
        tiles = [product[:, i * LANES : (i + 1) * LANES] for i in range(WIDTH // LANES)]
        product = (tiles[0] + tiles[1]) + (tiles[2] + tiles[3])
        upper_part = product.astype(BF16)
        lower_part = (product - upper_part.astype(F32)).astype(BF16)
        split = jnp.concatenate([upper_part, lower_part], axis=1)
        values = dot(picked, wqkv[2]).astype(BF16)
        for r in range(number * ROLES):
            rows = slice(r * ROWS, (r + 1) * ROWS)
            first = pl.multiple_of((t * ROLES + r) * HEADS, HEADS)
            scores[pl.ds(first, HEADS), 0:ROWS] = dot_nt(head_rows, split[rows])[0:HEADS]
            vals[t + r // ROLES, (r % ROLES) * LANES : (r % ROLES) * LANES + ROWS, :] = values[rows]

    def step(s, _):
        @pl.when(s < OWNERS)
        def _():
            for at, stages in STEPS.items():

                @pl.when(s == at)
                def _(stages=stages):
                    for awaited, sent in stages:
                        arrived(awaited)
                        for number in sent:
                            bl_copy(number).start()

            pick_rows(s)

        for after, begin, end in EARLY:

            @pl.when(s == after)
            def _(begin=begin, end=end):
                attend(begin, end)

        @pl.when(jnp.logical_and(jnp.logical_and(s >= LAG, s < OWNERS + LAG - 2), s % 2 == 1))
        def _():
            score_slots(s - LAG + 1, 2)

        @pl.when(jnp.logical_or(s == LAG - 1, s == OWNERS + LAG - 2))
        def _():
            score_slots((s // OWNERS) * (OWNERS - 1), 1)

        return 0

    lax.fori_loop(0, OWNERS + LAG - 1, step, 0)

    attend(*LAST)
    attended = sums[...].astype(BF16)
    emb_ref[...] = (blocks[0].astype(F32) + dot(attended, wout[1])).astype(BF16)

    finish(ev_out.at[pl.ds(1, OWNERS - 1)], ev_send.at[0])
    for ask in asks:
        ask.wait_send()
    finish(blocks.at[pl.ds(0, SENT_BLOCKS)], bl_send.at[0])
    finish(to_right, pk_send.at[0])
    finish(to_left, pk_send.at[1])


def hand_over(new_in, emb_in, new_ref, emb_ref):
    new_ref[...] = new_in[...]
    emb_ref[...] = emb_in[...]


def body(memory, features, dest, slot, neighbours, w_message, w_input, w_hidden, w_query, w_keyval, w_output):
    inside = pl.BlockSpec(memory_space=pltpu.VMEM)
    outside = pl.BlockSpec(memory_space=pl.ANY)
    vmem, dma = pltpu.VMEM, pltpu.SemaphoreType.DMA
    results = pl.pallas_call(
        kernel,
        out_shape=(
            jax.ShapeDtypeStruct((CELLS, WIDTH), BF16),
            jax.ShapeDtypeStruct((CELLS, WIDTH), BF16),
        ),
        in_specs=[outside, inside, outside, outside, outside, inside] + [outside] * 5,
        out_specs=(inside, inside),
        scratch_shapes=[
            vmem((CELLS, WIDTH), BF16),
            vmem((1, EVENTS), I32),
            vmem((1, EVENTS), I32),
            vmem((NBR, CELLS), I32),
            vmem((WIDTH, 3 * WIDTH), BF16),
            vmem((WIDTH, 3 * WIDTH), BF16),
            vmem((3, WIDTH, WIDTH), BF16),
            vmem((WIDTH, WIDTH), BF16),
            vmem((2, WIDTH, WIDTH), BF16),
            vmem((64, EVENTS), F32),
            vmem((64, WIDTH), F32),
            vmem((OWNERS, PACK, 128), BF16),
            vmem((OWNERS, PACK, 128), BF16),
            vmem((CELLS, 3 * WIDTH), F32),
            vmem((CELLS, WIDTH), F32),
            vmem((CELLS, LANES), F32),
            vmem((CELLS, WIDTH), BF16),
            vmem((2, 256, WIDTH), BF16),
            vmem((OWNERS, ROLES * ROWS, CELLS), BF16),
            vmem((OWNERS, ROLES * ROWS, CELLS), BF16),
            vmem((NBR, CELLS), I32),
            vmem((NBR, CELLS), I32),
            vmem((LANES, LANES), F32),
            vmem((2 * LANES, NBR * CELLS), BF16),
            vmem((LANES, LANES), BF16),
            vmem((2, LANES, LANES), BF16),
            vmem((BUCKETS, LANES), F32),
            vmem((OWNERS, CELLS, ROLES * LANES), BF16),
            vmem((2, HEADS, CELLS), F32),
            vmem((OWNERS, CELLS, WIDTH), BF16),
            vmem((OWNERS, ROLES * ROWS, WIDTH), BF16),
            vmem((OWNERS, ROWS, WIDTH), BF16),
            vmem((OWNERS, ROWS, WIDTH), BF16),
            vmem((CELLS, WIDTH), BF16),
            vmem((OWNERS, ROLES * LANES, WIDTH), BF16),
            vmem((BUCKETS * HEADS, LANES), F32),
            vmem((NBR, HEADS, CELLS), F32),
            vmem((2 * ROLES * HEADS, 2 * ROLES * LANES), BF16),
            dma((10,)),
            dma((1,)),
            dma((2,)),
            dma((2,)),
            dma((2,)),
            dma((1,)),
            dma((len(GROUPS),)),
            dma((2,)),
            dma((OWNERS // 2 + 1,)),
        ],
        compiler_params=pltpu.CompilerParams(
            collective_id=0, has_side_effects=True, vmem_limit_bytes=58 * 1024 * 1024
        ),
        cost_estimate=pl.CostEstimate(
            flops=12_000_000_000, bytes_accessed=6_000_000, transcendentals=2_000_000
        ),
    )(
        memory,
        features.T,
        dest.reshape(1, EVENTS),
        slot.reshape(1, EVENTS),
        neighbours.T,
        w_message,
        w_input,
        w_hidden,
        w_query,
        w_keyval,
        w_output,
    )
    return pl.pallas_call(
        hand_over,
        out_shape=(
            jax.ShapeDtypeStruct((CELLS, WIDTH), BF16),
            jax.ShapeDtypeStruct((CELLS, WIDTH), BF16),
        ),
        in_specs=[inside] * 2,
        out_specs=(inside, inside),
    )(*results)


def solution(mesh):
    rows = P(("group", "dev"), None)
    placed = (rows, rows, rows, P(("group", "dev")), rows) + (P(),) * 6
    return jax.shard_map(
        body, mesh=mesh, in_specs=placed, out_specs=(rows, rows), check_vma=False
    )
```
